128 devices in a mesh: role: 4 (over x), seq: 32 (over y, z, core).
Axes of the slice: x: 4, y: 4, z: 4, core: 2. Of those that a mesh axis runs over, the one named last changes fastest.
Arguments:
- cache_rows: bfloat16 [4, 131072, 576], P('role', 'seq'), may hold values from -6 to 6
- cache_request: int32 [4, 131072], P('role', 'seq'), may hold values from 0 to 2, never falling along the last dimension, each value on 1 to 87381 neighbouring positions
- sent_rows: bfloat16 [32768, 576], P(('role', 'seq')), may hold values from -6 to 6
- sent_owner: int32 [32768, 1], P(('role', 'seq')), may hold values from 0 to 127; in each aligned block of 256 rows (0 to 255, 256 to 511, ...) at most 4 rows name the same one
- sent_request: int32 [32768], P(('role', 'seq')), may hold values from 0 to 2
- new_rows: bfloat16 [4, 12, 576], P(None, 'role'), may hold values from -6 to 6
- query_nope: bfloat16 [4, 12, 128, 128], P(None, 'role', 'seq'), may hold values from -6 to 6
- query_rope: bfloat16 [4, 12, 128, 64], P(None, 'role', 'seq'), may hold values from -10 to 10
- absorb_key: bfloat16 [128, 128, 512], P('seq'), may hold values from -0.5 to 0.5
- absorb_value: bfloat16 [128, 512, 128], P('seq'), may hold values from -0.25 to 0.25
Outputs:
- attended: bfloat16 [4, 12, 128, 128], P(None, 'role', 'seq')
The draws below stay inside these ranges and needn't reach their ends.
Inputs may be any that keep to these rules, and one draw needn't show every extreme that they name: `sent_owner`: of the rows of one device, at most 4 have the same owner, and some owner gets exactly 4 of them. `cache_request`: within each group the request numbers never fall along the rows, every request has 1 to 87381 rows, and one has exactly that many.
All inputs are finite; a program needn't handle non-finite values.
Results may differ from the reference program's by a relative error of at most 0.012.
Values may be sent and summed in bfloat16 or wider, within the bound.
A program may use at most 256 MiB of HBM per device.

```python
import math
import jax
import jax.numpy as jnp
import numpy as np
from jax import lax

H = 128
DN = 128
DR = 64
DC = 512
DV = 128
KW = 576
REQ = 3
STEPS = 4
L_DEV = 4096
SEND = 256
CAP = 4
N_ROLE = 4
N_SEQ = 32
DEVICES = 128


def draw_cache_rows(key, part):
    seeded = jax.random.fold_in(key, 11)
    values = jax.random.truncated_normal(seeded, -6.0, 6.0, (N_ROLE, N_SEQ * L_DEV, KW), jnp.float32)
    return values.astype(jnp.bfloat16)


def draw_sent_rows(key, part):
    seeded = jax.random.fold_in(key, 12)
    values = jax.random.truncated_normal(seeded, -6.0, 6.0, (DEVICES * SEND, KW), jnp.float32)
    return values.astype(jnp.bfloat16)


def draw_new_rows(key, part):
    seeded = jax.random.fold_in(key, 13)
    values = jax.random.truncated_normal(seeded, -6.0, 6.0, (STEPS, N_ROLE * REQ, KW), jnp.float32)
    return values.astype(jnp.bfloat16)


def draw_query_rope(key, part):
    seeded = jax.random.fold_in(key, 14)
    values = jax.random.truncated_normal(seeded, -6.0, 6.0, (STEPS, N_ROLE * REQ, H, DR), jnp.float32)
    return values.astype(jnp.bfloat16)


def place_ends(array, own_key, least, largest):
    longest = array.shape.index(max(array.shape))
    spots = []
    for shift in (0, 1):
        where = [jax.random.randint(jax.random.fold_in(own_key, axis), (), 0, length) for axis, length in enumerate(array.shape)]
        where[longest] = (where[longest] + shift) % array.shape[longest]
        spots.append(tuple(where))
    return array.at[spots[0]].set(least).at[spots[1]].set(largest)


def levels(rng, dims, cuts, smallest, high):
    def one(position, shards_of):
        heights = jax.random.uniform(jax.random.fold_in(jax.random.fold_in(rng, 6), position), (shards_of,), jnp.float32, smallest / len(cuts), high / len(cuts))
        return jnp.repeat(jnp.exp(heights), dims[position] // shards_of).reshape((-1,) + (1,) * (len(dims) - position - 1))

    loudness = one(*cuts[0])
    for cut in cuts[1:]:
        loudness = loudness * one(*cut)
    return loudness


def length_profile(amount, total, most, slope):
    weights = [(1 << 20) // math.isqrt(grade ** slope) + 1 for grade in range(2, amount + 1)]
    surplus, counts = total - most - (amount - 1), [1] * (amount - 1)
    while surplus > 0:
        candidates = [i for i in range(amount - 1) if counts[i] < most]
        pool, left = sum([weights[i] for i in candidates]), surplus
        for i in candidates:
            addition = min(most - counts[i], max(1, left * weights[i] // pool), surplus)
            counts[i] = counts[i] + addition
            surplus = surplus - addition
    return np.array([most] + counts)


def ragged(own_key, amount, total, reach, slope):
    if amount == 2:
        one = jax.random.randint(own_key, (), max(1, total - reach), min(reach, total - 1) + 1)
        return jnp.stack([one, total - one])
    sizes = jnp.asarray(length_profile(amount, total, reach, slope), jnp.int32)
    couples = (amount - 1) // 2
    donor, receiver = sizes[1:1 + 2 * couples:2], sizes[2:2 + 2 * couples:2]
    room = jnp.minimum(donor - 1, reach - receiver)
    shifted = jax.random.randint(jax.random.fold_in(own_key, 1), (couples,), 0, 1 << 20) % (room + 1)
    sizes = sizes.at[1:1 + 2 * couples:2].set(donor - shifted).at[2:2 + 2 * couples:2].set(receiver + shifted)
    return sizes[jax.random.permutation(jax.random.fold_in(own_key, 2), amount)]


def routed_block(stream_key, own, number, rows, amount, top, limit, skew):
    ranking = jax.random.permutation(stream_key, amount)
    heavy_load, usual = portions_of(amount, rows * top, limit, skew, True), portions_of(amount, rows * top, limit, skew, False)
    places = jnp.arange(amount)

    def named(tallies, offset_by):
        used = int((tallies > 0).sum())
        fixed = max(1, used // 4)
        shifted = fixed + (places - fixed + offset_by * (used - fixed)) % max(1, amount - fixed)
        return jnp.zeros((amount,), jnp.int32).at[ranking[jnp.where(places < fixed, places, shifted)]].set(jnp.asarray(tallies, jnp.int32))

    tallies = jnp.where(number % 4 == 0, named(heavy_load, number // 4), named(usual, number - number // 4 - 1))
    mixed = jax.random.permutation(jax.random.fold_in(own, 3), amount)
    donor, receiver = mixed[0:amount // 2 * 2:2], mixed[1:amount // 2 * 2:2]
    room = jnp.minimum(tallies[donor] - 1, limit - tallies[receiver]) // 2
    room = jnp.where((donor == ranking[0]) | (receiver == ranking[0]) | (tallies[receiver] == 0), 0, jnp.maximum(room, 0))
    shifted = jax.random.randint(jax.random.fold_in(own, 4), (amount // 2,), 0, 1 << 20) % (room + 1)
    tallies = tallies.at[donor].add(-shifted).at[receiver].add(shifted)
    members = jnp.searchsorted(jnp.cumsum(tallies), jnp.arange(rows * top), side="right").astype(jnp.int32)
    table = members.reshape(top, rows).T
    table = table[jax.random.permutation(jax.random.fold_in(own, 1), rows)]
    offset_by = jax.random.randint(jax.random.fold_in(own, 2), (rows, 1), 0, top)
    return jnp.take_along_axis(table, (jnp.arange(top)[None, :] + offset_by) % top, axis=1)


def portions_of(number_of, total, reach, lean, full):
    weights = [(1 << 20) // math.isqrt(grade ** lean) + 1 for grade in range(1, number_of + 1)]
    largest = reach if full else min(reach, max(-(-total // number_of), total * weights[0] // sum(weights)))
    least = 1 if total - largest >= number_of - 1 else 0
    holding, surplus = [largest] + [least] * (number_of - 1), total - largest - least * (number_of - 1)
    while surplus > 0:
        candidates = [i for i in range(1, number_of) if holding[i] < largest] or [i for i in range(1, number_of) if holding[i] < reach]
        mass, remaining = sum([weights[i] for i in candidates]), surplus
        for i in candidates:
            more = min(reach - holding[i], max(1, remaining * weights[i] // mass), surplus)
            holding[i] = holding[i] + more
            surplus = surplus - more
    return np.array(holding)


def centred(rng, extent, width, reach, split=(), dtype=jnp.bfloat16):
    level = levels(rng, extent, split, -0.22, 0.18) if split else 1.0
    values = jax.random.normal(rng, extent, jnp.float32) * width * level
    return jnp.minimum(jnp.maximum(values, -reach), reach).astype(dtype)


def setup_inputs(seed: int = 0) -> dict:
    key_list = jax.random.split(jax.random.key(seed), 11)
    cache_rows = draw_cache_rows(jax.random.fold_in(key_list[10], 71), 0)
    cache_request = jax.vmap(lambda own: jnp.searchsorted(jnp.cumsum(ragged(own, REQ, N_SEQ * L_DEV, 2 * N_SEQ * L_DEV // REQ, 2)), jnp.arange(N_SEQ * L_DEV), side="right"))(jax.random.split(key_list[1], N_ROLE)).reshape((N_ROLE, N_SEQ * L_DEV)).astype(jnp.int32)
    sent_rows = draw_sent_rows(jax.random.fold_in(key_list[10], 71), 0)
    sent_owner_keys = jax.random.split(jax.random.fold_in(key_list[3], 1), (DEVICES * SEND) // SEND)
    sent_owner_turns = jax.random.permutation(jax.random.fold_in(key_list[3], 3), (DEVICES * SEND) // SEND)
    sent_owner = jax.vmap(lambda own, number: routed_block(jax.random.fold_in(key_list[3], 2), own, number, SEND, DEVICES, 1, CAP, 2))(sent_owner_keys, sent_owner_turns).reshape((DEVICES * SEND, 1))
    sent_request = place_ends(jax.random.randint(key_list[4], (DEVICES * SEND,), 0, REQ), jax.random.fold_in(key_list[4], 1), 0, REQ - 1).astype(jnp.int32)
    new_rows = draw_new_rows(jax.random.fold_in(key_list[10], 71), 0)
    query_nope = centred(key_list[6], (STEPS, N_ROLE * REQ, H, DN), 1.0, 6.0, ((1, 4), (2, 32)))
    query_rope = draw_query_rope(jax.random.fold_in(key_list[10], 71), 0)
    absorb_key = centred(key_list[8], (H, DN, DC), DN ** -0.5, 0.5, ((0, 32),))
    absorb_value = centred(key_list[9], (H, DC, DV), DC ** -0.5, 0.25, ((0, 32),))
    return {"cache_rows": cache_rows, "cache_request": cache_request, "sent_rows": sent_rows, "sent_owner": sent_owner, "sent_request": sent_request, "new_rows": new_rows, "query_nope": query_nope, "query_rope": query_rope, "absorb_key": absorb_key, "absorb_value": absorb_value}


BLOCK = 2048
FAR = -1e30


def join(first, second):
    top = jnp.maximum(first[0], second[0])
    a = jnp.exp(first[0] - top)
    b = jnp.exp(second[0] - top)
    return (top, first[1] * a + second[1] * b, first[2] * a[..., None] + second[2] * b[..., None])


def reference(cache_rows, cache_request, sent_rows, sent_owner, sent_request, new_rows, query_nope, query_rope, absorb_key, absorb_value):
    scale = 1.0 / ((DN + DR) ** 0.5)
    q_latent = jnp.einsum("trhn,hnc->trhc", query_nope.astype(jnp.float32), absorb_key.astype(jnp.float32)).astype(jnp.bfloat16)
    query = jnp.concatenate([q_latent, query_rope], axis=-1)
    owner_group = sent_owner[:, 0] // N_SEQ
    total = N_SEQ * L_DEV + DEVICES * SEND
    extra = (-total) % BLOCK
    steps_idx = jnp.arange(STEPS)
    causal = steps_idx[:, None] >= steps_idx[None, :]
    results = []
    for group in range(N_ROLE):
        keys = jnp.concatenate([cache_rows[group], sent_rows], axis=0)
        ids = jnp.concatenate([cache_request[group], jnp.where(owner_group == group, sent_request, -1)]).astype(jnp.int32)
        order = jnp.argsort(ids, stable=True)
        keys_sorted = jnp.concatenate([keys[order], jnp.zeros((extra, KW), jnp.bfloat16)], axis=0)
        ids_sorted = jnp.concatenate([ids[order], jnp.full((extra,), REQ, jnp.int32)]).astype(jnp.int32)
        outs = []
        for request in range(REQ):
            row = group * REQ + request
            q_rows = query[:, row].reshape(STEPS * H, KW)
            start = jnp.sum(ids_sorted < request).astype(jnp.int32)
            stop = jnp.sum(ids_sorted <= request).astype(jnp.int32)

            def step_block(i, carry):
                k_block = lax.dynamic_slice_in_dim(keys_sorted, (i * BLOCK).astype(jnp.int32), BLOCK, 0)
                i_block = lax.dynamic_slice_in_dim(ids_sorted, (i * BLOCK).astype(jnp.int32), BLOCK, 0)
                valid = (i_block == request)[None, :]
                score = lax.dot_general(q_rows, k_block, (((1,), (1,)), ((), ())), preferred_element_type=jnp.float32) * scale
                top = jnp.max(jnp.where(valid, score, FAR), axis=1)
                expo = jnp.where(valid, jnp.exp(score - top[:, None]), 0.0)
                part = (top, jnp.sum(expo, axis=1), jnp.dot(expo.astype(jnp.bfloat16), k_block[:, :DC], preferred_element_type=jnp.float32))
                return join(carry, part)

            init = (jnp.full((STEPS * H,), FAR, jnp.float32), jnp.zeros((STEPS * H,), jnp.float32), jnp.zeros((STEPS * H, DC), jnp.float32))
            first = (start // BLOCK).astype(jnp.int32)
            last = ((stop + BLOCK - 1) // BLOCK).astype(jnp.int32)
            top, tot, acc = lax.fori_loop(first, last, step_block, init)
            cached = (top.reshape(STEPS, H), tot.reshape(STEPS, H), acc.reshape(STEPS, H, DC))
            fresh = new_rows[:, row]
            q_step = query[:, row]
            score = jnp.einsum("thk,uk->thu", q_step.astype(jnp.float32), fresh.astype(jnp.float32)) * scale
            mask = causal[:, None, :]
            top2 = jnp.max(jnp.where(mask, score, FAR), axis=2)
            expo = jnp.where(mask, jnp.exp(score - top2[..., None]), 0.0)
            acc2 = jnp.einsum("thu,uc->thc", expo.astype(jnp.bfloat16).astype(jnp.float32), fresh[:, :DC].astype(jnp.float32))
            top, tot, acc = join(cached, (top2, jnp.sum(expo, axis=2), acc2))
            latent_out = (acc / tot[..., None]).astype(jnp.bfloat16)
            outs.append(jnp.einsum("thc,hcv->thv", latent_out.astype(jnp.float32), absorb_value.astype(jnp.float32)).astype(jnp.bfloat16))
        results.append(jnp.stack(outs, axis=1))
    return jnp.concatenate(results, axis=1)
```

```python
import functools

import jax
import jax.numpy as jnp
from jax import lax
from jax.experimental import pallas as pl
from jax.experimental.pallas import tpu as pltpu
from jax.sharding import PartitionSpec as P

FAR = -1e30
LOG2E = 1.4426950408889634
MESH = pl.DeviceIdType.MESH
F32 = jnp.float32
BF16 = jnp.bfloat16
NT = (((1,), (1,)), ((), ()))

CAP = 4
SPAN = 512
VMEM_BYTES = 56 * 1024 * 1024


def iota(shape, dim):
    return lax.broadcasted_iota(jnp.int32, shape, dim)


def place(side):
    seq = lax.axis_index("seq")
    return lax.div(seq, 2 * side), lax.rem(lax.div(seq, 2), side), lax.rem(seq, 2)


def seq_of(side, y, z, c):
    return (y * side + z) * 2 + c


def turned(value, by, size):
    return lax.rem(value + by, size)


def start_together(devices):
    barrier = pltpu.get_barrier_semaphore()
    for device in devices:
        pl.semaphore_signal(barrier, inc=1, device_id=device, device_id_type=MESH)
    pl.semaphore_wait(barrier, len(devices))


def absorb_queries(nope_ref, rope_ref, key_ref):
    rows = nope_ref.shape[0]
    heads = key_ref.shape[0]
    head = lax.rem(iota((rows, 1), 0), heads)
    total = jnp.zeros((rows, key_ref.shape[2]), F32)
    for h in range(heads):
        part = jnp.dot(nope_ref[...], key_ref[h], preferred_element_type=F32)
        total = total + jnp.where(head == h, part, 0.0)
    return total.astype(BF16)


def exchange_kernel(
    side,
    n_role,
    nope_ref,
    rope_ref,
    key_ref,
    rows_ref,
    owner_ref,
    request_ref,
    qa_ref,
    qb_ref,
    got_ref,
    tag_ref,
    own_a,
    own_b,
    packed,
    tags,
    send_sem,
    recv_sem,
    local_sem,
):
    g = lax.axis_index("role")
    seq = lax.axis_index("seq")
    y, z, c = place(side)
    y_peers = [{"role": g, "seq": seq_of(side, turned(y, d, side), z, c)} for d in range(1, side)]
    z_peers = [{"role": g, "seq": seq_of(side, y, turned(z, d, side), c)} for d in range(1, side)]
    x_peers = [{"role": turned(g, d, n_role), "seq": seq} for d in range(1, n_role)]
    mate = {"role": g, "seq": seq_of(side, y, z, 1 - c)}
    start_together(y_peers + z_peers + x_peers + [mate])

    count = [0]

    def send(src, dst, device):
        k = count[0]
        count[0] += 1
        copy = pltpu.make_async_remote_copy(
            src_ref=src,
            dst_ref=dst,
            send_sem=send_sem.at[k],
            recv_sem=recv_sem.at[k],
            device_id=device,
            device_id_type=MESH,
        )
        copy.start()
        return copy

    q_latent = absorb_queries(nope_ref, rope_ref, key_ref)
    half = own_a.shape[1]
    own_a[...] = q_latent[:, :half]
    own_b[:, : q_latent.shape[1] - half] = q_latent[:, half:]
    own_b[:, q_latent.shape[1] - half :] = rope_ref[...]

    first_a = [send(own_a, qa_ref.at[c, y, z], peer) for peer in y_peers]
    first_b = [send(own_b, qb_ref.at[c, y, z], peer) for peer in z_peers]
    keep_a = pltpu.make_async_copy(own_a, qa_ref.at[c, y, z], local_sem.at[0])
    keep_b = pltpu.make_async_copy(own_b, qb_ref.at[c, y, z], local_sem.at[1])
    keep_a.start()
    keep_b.start()

    send_count = rows_ref.shape[0]
    devices = n_role * 2 * side * side
    owner = owner_ref[...]
    hits = iota((devices, send_count), 0) == owner
    earlier = iota((send_count, send_count), 0) < iota((send_count, send_count), 1)
    before = jnp.dot(hits.astype(BF16), earlier.astype(BF16), preferred_element_type=F32)
    slot = jnp.sum(jnp.where(hits, before, 0.0), axis=0, keepdims=True).astype(jnp.int32)
    position = owner * CAP + slot
    chosen = (iota((devices * CAP, send_count), 0) == position).astype(BF16)
    room = packed.shape[1]
    packed[...] = (
        jnp.dot(chosen, rows_ref[...], preferred_element_type=F32)
        .astype(BF16)
        .reshape(packed.shape)
    )
    marks = jnp.broadcast_to((request_ref[...] + 1).astype(BF16), (8, send_count))
    tag_rows = lax.dot_general(marks, chosen, NT, preferred_element_type=F32)
    for i in range(n_role):
        tags[i] = tag_rows[:, i * room : (i + 1) * room]

    crossing = []
    for d in range(1, n_role):
        there = turned(g, d, n_role)
        crossing.append(send(packed.at[there], got_ref.at[g], x_peers[d - 1]))
        crossing.append(send(tags.at[there], tag_ref.at[g], x_peers[d - 1]))
    keep_rows = pltpu.make_async_copy(packed.at[g], got_ref.at[g], local_sem.at[2])
    keep_tags = pltpu.make_async_copy(tags.at[g], tag_ref.at[g], local_sem.at[3])
    keep_rows.start()
    keep_tags.start()

    keep_a.wait()
    for copy in first_a:
        copy.wait_recv()
    line_a = qa_ref.at[c, :, z]
    second_a = [send(line_a, line_a, peer) for peer in z_peers]
    last = [send(line_a, line_a, mate)]
    keep_b.wait()
    for copy in first_b:
        copy.wait_recv()
    line_b = qb_ref.at[c, y]
    second_b = [send(line_b, line_b, peer) for peer in y_peers]
    last.append(send(line_b, line_b, mate))
    for d in range(1, side):
        second_a[d - 1].wait_recv()
        line = qa_ref.at[c, :, turned(z, side - d, side)]
        last.append(send(line, line, mate))
        second_b[d - 1].wait_recv()
        line = qb_ref.at[c, turned(y, side - d, side)]
        last.append(send(line, line, mate))

    keep_rows.wait()
    keep_tags.wait()
    for copy in crossing + last:
        copy.wait_recv()
    for copy in first_a + first_b + crossing + second_a + second_b + last:
        copy.wait_send()


def attend_kernel(
    scale,
    cache_ref,
    ids_ref,
    got_ref,
    tag_ref,
    qa_ref,
    qb_ref,
    aa_ref,
    ab_ref,
    st_ref,
    keys,
    extra,
    top_s,
    tot_s,
    acc_s,
    sems,
):
    chunks = sems.shape[0]
    rows = cache_ref.shape[1]
    part = rows // chunks
    copies = []
    for i in range(chunks):
        copy = pltpu.make_async_copy(
            cache_ref.at[0, pl.ds(i * part, part)], keys.at[pl.ds(i * part, part)], sems.at[i]
        )
        copy.start()
        copies.append(copy)

    sources, per = tag_ref.shape[0], tag_ref.shape[2]
    room = sources * per
    tag = jnp.concatenate([tag_ref[i, 0:1, :] for i in range(sources)], axis=1)
    requests = qa_ref.shape[1] // 16
    kinds = iota((8, room), 0)
    same = jnp.where(kinds == requests, 0.0, (kinds + 1).astype(F32)) == tag
    same = same & (kinds <= requests)
    same_f = same.astype(F32)
    earlier = (iota((room, room), 0) < iota((room, room), 1)).astype(BF16)
    before = jnp.dot(same_f.astype(BF16), earlier, preferred_element_type=F32)
    counts = [jnp.sum(same_f[b]).astype(jnp.int32) for b in range(requests)]
    starts = [jnp.int32(0)]
    for b in range(requests):
        starts.append(starts[-1] + counts[b])
    offset = jnp.zeros((8, room), F32)
    for b in range(requests + 1):
        offset = jnp.where(kinds == b, starts[b].astype(F32), offset)
    rank = jnp.sum(jnp.where(same, before + offset, 0.0), axis=0, keepdims=True).astype(jnp.int32)
    moved = (iota((room, room), 0) == rank).astype(BF16)
    flat = got_ref[...].reshape(room, got_ref.shape[2])
    extra[...] = jnp.dot(moved, flat, preferred_element_type=F32).astype(BF16)

    ids = ids_ref[...]
    edges = [jnp.int32(0)]
    for b in range(1, requests):
        edges.append(jnp.sum((ids < b).astype(jnp.int32)))
    edges.append(jnp.int32(rows))

    for copy in copies:
        copy.wait()

    count = top_s.shape[0]
    half_q = count // 2
    width_a = qa_ref.shape[2]
    factor = scale * LOG2E
    latent = acc_s.shape[1]
    units = qa_ref.shape[0]
    lane = iota((count, 128), 1)
    row = lax.rem(iota((count, 128), 0), 16)
    top_rows = jnp.zeros((units, 128), F32)
    tot_rows = jnp.zeros((units, 128), F32)

    for b in range(requests):
        top_s[...] = jnp.full(top_s.shape, FAR, F32)
        tot_s[...] = jnp.zeros(tot_s.shape, F32)
        acc_s[...] = jnp.zeros(acc_s.shape, F32)

        def visit(key_block, lower, upper, width):
            columns = iota((1, width), 1)
            inside = (columns >= lower) & (columns < upper)
            for t in range(2):
                here = pl.ds(t * half_q, half_q)
                q_here = pl.ds(t * (units // 2), units // 2)
                qa = qa_ref[q_here, b * 16 : (b + 1) * 16, :].reshape(half_q, width_a)
                qb = qb_ref[q_here, b * 16 : (b + 1) * 16, :].reshape(half_q, qb_ref.shape[2])
                score = lax.dot_general(qa, key_block[:, :width_a], NT, preferred_element_type=F32)
                score += lax.dot_general(qb, key_block[:, width_a:], NT, preferred_element_type=F32)
                score = jnp.where(inside, score * factor, FAR)
                old = top_s[here]
                top = jnp.maximum(old, jnp.max(score, axis=1, keepdims=True))
                expo = jnp.exp2(score - top)
                keep = jnp.exp2(old - top)
                top_s[here] = top
                tot_s[here] = tot_s[here] * keep + jnp.sum(expo, axis=1, keepdims=True)
                acc_s[here] = acc_s[here] * keep + jnp.dot(
                    expo.astype(BF16), key_block[:, :latent], preferred_element_type=F32
                )

        def over(source, lower, upper, width):
            def body(i, _):
                begin = pl.multiple_of(i * width, width)
                visit(source[pl.ds(begin, width), :], lower - begin, upper - begin, width)
                return 0

            lax.fori_loop(lax.div(lower, width), lax.div(upper + (width - 1), width), body, 0)

        over(keys, edges[b], edges[b + 1], SPAN)
        over(extra, starts[b], starts[b + 1], 256)

        for u in range(units):
            piece = acc_s[u * 16 : (u + 1) * 16, :].astype(BF16)
            aa_ref[u, b * 16 : (b + 1) * 16, :] = piece[:, : latent // 2]
            ab_ref[u, b * 16 : (b + 1) * 16, :] = piece[:, latent // 2 :]
        mine = lane == row + b * 16
        top_rows += jnp.sum(jnp.where(mine, top_s[...], 0.0).reshape(units, 16, 128), axis=1)
        tot_rows += jnp.sum(jnp.where(mine, tot_s[...], 0.0).reshape(units, 16, 128), axis=1)
    st_ref[:, 0, :] = top_rows
    st_ref[:, 1, :] = tot_rows


def blend(tops):
    top = functools.reduce(jnp.maximum, tops)
    return top, [jnp.exp2(item - top) for item in tops]


def columns_of(weight, rows):
    n = weight.shape[0]
    pick = iota((n, rows, 128), 2) == iota((n, rows, 128), 1)
    return jnp.sum(jnp.where(pick, weight[:, None, :], 0.0), axis=2, keepdims=True)


def total_of(tots, weights):
    return functools.reduce(jnp.add, [t * w for t, w in zip(tots, weights)])


def acc_of(accs, columns):
    return functools.reduce(jnp.add, [a.astype(F32) * col for a, col in zip(accs, columns)])


def combine_kernel(
    side,
    scale,
    aa_ref,
    ab_ref,
    st_ref,
    qa_ref,
    qb_ref,
    new_ref,
    value_ref,
    out_ref,
    own_a,
    own_b,
    mine_a,
    mine_b,
    mine_st,
    pair_a,
    pair_b,
    pair_st,
    mid_a,
    mid_b,
    mid_st,
    in1_a,
    in1_b,
    in1_sa,
    in1_sb,
    mid2_a,
    mid2_b,
    mid2_sa,
    mid2_sb,
    in2_a,
    in2_b,
    in2_sa,
    in2_sb,
    send_sem,
    recv_sem,
    local_sem,
):
    g = lax.axis_index("role")
    y, z, c = place(side)
    y_peers = [{"role": g, "seq": seq_of(side, turned(y, d, side), z, c)} for d in range(1, side)]
    z_peers = [{"role": g, "seq": seq_of(side, y, turned(z, d, side), c)} for d in range(1, side)]
    mate = {"role": g, "seq": seq_of(side, y, z, 1 - c)}

    keep = [
        pltpu.make_async_copy(aa_ref.at[c], mine_a, local_sem.at[0]),
        pltpu.make_async_copy(ab_ref.at[c], mine_b, local_sem.at[1]),
        pltpu.make_async_copy(st_ref.at[c], mine_st, local_sem.at[2]),
        pltpu.make_async_copy(qa_ref.at[c, y, z], own_a, local_sem.at[3]),
        pltpu.make_async_copy(qb_ref.at[c, y, z], own_b, local_sem.at[4]),
    ]
    for copy in keep:
        copy.start()
    start_together(y_peers + z_peers + [mate])

    count = [0]

    def send(src, dst, device):
        k = count[0]
        count[0] += 1
        copy = pltpu.make_async_remote_copy(
            src_ref=src,
            dst_ref=dst,
            send_sem=send_sem.at[k],
            recv_sem=recv_sem.at[k],
            device_id=device,
            device_id_type=MESH,
        )
        copy.start()
        return copy

    across = [
        send(aa_ref.at[1 - c], pair_a, mate),
        send(ab_ref.at[1 - c], pair_b, mate),
        send(st_ref.at[1 - c], pair_st, mate),
    ]
    for copy in keep:
        copy.wait()

    half = own_a.shape[1]
    rows = own_a.shape[0]
    latent = value_ref.shape[1]
    new = new_ref[...]
    score = lax.dot_general(own_a[...], new[:, :half], NT, preferred_element_type=F32)
    score += lax.dot_general(own_b[...], new[:, half:], NT, preferred_element_type=F32)
    score = score * (scale * LOG2E)
    fresh = new.shape[0]
    requests = rows // 16
    heads = value_ref.shape[0]
    r_row, r_col = iota((rows, fresh), 0), iota((rows, fresh), 1)
    seen = (lax.div(r_row, 16) == lax.rem(r_col, requests)) & (
        lax.div(lax.rem(r_row, 16), heads) >= lax.div(r_col, requests)
    )
    top0 = jnp.max(jnp.where(seen, score, FAR), axis=1, keepdims=True)
    expo = jnp.where(seen, jnp.exp2(score - top0), 0.0)
    tot0 = jnp.sum(expo, axis=1, keepdims=True)
    acc0 = jnp.dot(expo.astype(BF16), new[:, :latent], preferred_element_type=F32)

    for copy in across:
        copy.wait_recv()
    for i in range(side):
        top, weights = blend([mine_st[i, :, 0, :], pair_st[i, :, 0, :]])
        columns = [columns_of(w, rows) for w in weights]
        mid_st[i, :, 0, :] = top
        mid_st[i, :, 1, :] = total_of([mine_st[i, :, 1, :], pair_st[i, :, 1, :]], weights)
        mid_a[i] = acc_of([mine_a[i], pair_a[i]], columns).astype(BF16)
        mid_b[i] = acc_of([mine_b[i], pair_b[i]], columns).astype(BF16)

    over_a, over_b = [], []
    for d in range(1, side):
        there_y, there_z = turned(y, d, side), turned(z, d, side)
        over_a.append(send(mid_a.at[there_y], in1_a.at[d - 1], y_peers[d - 1]))
        over_a.append(send(mid_st.at[there_y], in1_sa.at[d - 1], y_peers[d - 1]))
        over_b.append(send(mid_b.at[:, there_z], in1_b.at[d - 1], z_peers[d - 1]))
        over_b.append(send(mid_st.at[:, there_z], in1_sb.at[d - 1], z_peers[d - 1]))

    def settle(copies, mine_acc, mine_stat, in_acc, in_stat):
        for copy in copies:
            copy.wait_recv()
        stats = [mine_stat] + [in_stat[d] for d in range(side - 1)]
        top, weights = blend([s[:, 0, :] for s in stats])
        columns = [columns_of(w, rows) for w in weights]
        total = total_of([s[:, 1, :] for s in stats], weights)
        acc = acc_of([mine_acc] + [in_acc[d] for d in range(side - 1)], columns)
        return top, total, acc

    top, total, acc = settle(over_a, mid_a[y], mid_st[y], in1_a, in1_sa)
    mid2_sa[:, 0, :] = top
    mid2_sa[:, 1, :] = total
    mid2_a[...] = acc.astype(BF16)
    next_a = []
    for d in range(1, side):
        there = turned(z, d, side)
        next_a.append(send(mid2_a.at[there], in2_a.at[d - 1], z_peers[d - 1]))
        next_a.append(send(mid2_sa.at[there], in2_sa.at[d - 1], z_peers[d - 1]))
    top, total, acc = settle(over_b, mid_b[:, z], mid_st[:, z], in1_b, in1_sb)
    mid2_sb[:, 0, :] = top
    mid2_sb[:, 1, :] = total
    mid2_b[...] = acc.astype(BF16)
    next_b = []
    for d in range(1, side):
        there = turned(y, d, side)
        next_b.append(send(mid2_b.at[there], in2_b.at[d - 1], y_peers[d - 1]))
        next_b.append(send(mid2_sb.at[there], in2_sb.at[d - 1], y_peers[d - 1]))

    def finish(copies, mine_acc, mine_stat, in_acc, in_stat, fresh_acc):
        for copy in copies:
            copy.wait_recv()
        stats = [mine_stat] + [in_stat[d] for d in range(side - 1)]
        top, weights = blend([s[0:1, :] for s in stats])
        columns = [columns_of(w, rows)[0] for w in weights]
        total = total_of([s[1:2, :] for s in stats], weights)
        acc = acc_of([mine_acc] + [in_acc[d] for d in range(side - 1)], columns)
        top_c, tot_c = columns_of(top, rows)[0], columns_of(total, rows)[0]
        best = jnp.maximum(top_c, top0)
        keep_c, keep_0 = jnp.exp2(top_c - best), jnp.exp2(top0 - best)
        tot = tot_c * keep_c + tot0 * keep_0
        return ((acc * keep_c + fresh_acc * keep_0) / tot).astype(BF16)

    out_a = finish(next_a, mid2_a[z], mid2_sa[z], in2_a, in2_sa, acc0[:, : latent // 2])
    out_b = finish(next_b, mid2_b[y], mid2_sb[y], in2_b, in2_sb, acc0[:, latent // 2 :])
    head = lax.rem(iota((rows, 1), 0), heads)
    result = jnp.zeros(out_ref.shape, F32)
    for h in range(heads):
        part = jnp.dot(out_a, value_ref[h, : latent // 2], preferred_element_type=F32)
        part += jnp.dot(out_b, value_ref[h, latent // 2 :], preferred_element_type=F32)
        result = result + jnp.where(head == h, part, 0.0)
    out_ref[...] = result.astype(BF16)

    for copy in across + over_a + over_b + next_a + next_b:
        copy.wait_send()


def per_device(
    cache_rows,
    cache_request,
    sent_rows,
    sent_owner,
    sent_request,
    new_rows,
    query_nope,
    query_rope,
    absorb_key,
    absorb_value,
):
    n_role = lax.axis_size("role")
    n_seq = lax.axis_size("seq")
    side = 1
    while 2 * side * side < n_seq:
        side += 1
    steps, requests, heads, nope = query_nope.shape
    rope = query_rope.shape[3]
    latent = absorb_key.shape[2]
    width = sent_rows.shape[1]
    half = latent // 2
    own = steps * requests * heads
    send = sent_rows.shape[0]
    room = CAP * n_seq
    scale = 1.0 / float(nope + rope) ** 0.5
    local_rows = cache_rows.shape[1]

    x_nope = jnp.transpose(query_nope, (1, 0, 2, 3)).reshape(own, nope)
    x_rope = jnp.transpose(query_rope, (1, 0, 2, 3)).reshape(own, rope)
    fresh = new_rows.reshape(steps * requests, width)

    vmem = pl.BlockSpec(memory_space=pltpu.VMEM)
    hbm = pl.BlockSpec(memory_space=pl.ANY)
    dma = pltpu.SemaphoreType.DMA

    copies = 4 * (side - 1) + 2 * (n_role - 1) + 2 * side
    qa, qb, got, tags = pl.pallas_call(
        functools.partial(exchange_kernel, side, n_role),
        out_shape=(
            jax.ShapeDtypeStruct((2, side, side, own, half), BF16),
            jax.ShapeDtypeStruct((2, side, side, own, width - half), BF16),
            jax.ShapeDtypeStruct((n_role, room, width), BF16),
            jax.ShapeDtypeStruct((n_role, 8, room), F32),
        ),
        in_specs=[vmem] * 6,
        out_specs=(hbm, hbm, hbm, hbm),
        scratch_shapes=[
            pltpu.VMEM((own, half), BF16),
            pltpu.VMEM((own, width - half), BF16),
            pltpu.VMEM((n_role, room, width), BF16),
            pltpu.VMEM((n_role, 8, room), F32),
            dma((copies,)),
            dma((copies,)),
            dma((4,)),
        ],
        compiler_params=pltpu.CompilerParams(
            collective_id=0, has_side_effects=True, vmem_limit_bytes=VMEM_BYTES
        ),
        name="exchange",
    )(x_nope, x_rope, absorb_key, sent_rows, sent_owner.reshape(1, send), sent_request.reshape(1, send))

    units = 2 * side * side
    count = units * steps * heads
    acc_a, acc_b, stats = pl.pallas_call(
        functools.partial(attend_kernel, scale),
        out_shape=(
            jax.ShapeDtypeStruct((units, own, half), BF16),
            jax.ShapeDtypeStruct((units, own, half), BF16),
            jax.ShapeDtypeStruct((units, 2, 128), F32),
        ),
        in_specs=[hbm, vmem, vmem, vmem, vmem, vmem],
        out_specs=(vmem, vmem, vmem),
        scratch_shapes=[
            pltpu.VMEM((local_rows, width), BF16),
            pltpu.VMEM((n_role * room, width), BF16),
            pltpu.VMEM((count, 1), F32),
            pltpu.VMEM((count, 1), F32),
            pltpu.VMEM((count, latent), F32),
            dma((4,)),
        ],
        compiler_params=pltpu.CompilerParams(vmem_limit_bytes=VMEM_BYTES),
        name="attend",
    )(
        cache_rows,
        cache_request,
        got,
        tags,
        qa.reshape(units, own, half),
        qb.reshape(units, own, width - half),
    )

    grid = (side, side)
    copies = 3 + 8 * (side - 1)
    out = pl.pallas_call(
        functools.partial(combine_kernel, side, scale),
        out_shape=jax.ShapeDtypeStruct((own, absorb_value.shape[2]), BF16),
        in_specs=[hbm] * 5 + [vmem] * 2,
        out_specs=vmem,
        scratch_shapes=[
            pltpu.VMEM((own, half), BF16),
            pltpu.VMEM((own, width - half), BF16),
            pltpu.VMEM(grid + (own, half), BF16),
            pltpu.VMEM(grid + (own, half), BF16),
            pltpu.VMEM(grid + (2, 128), F32),
            pltpu.VMEM(grid + (own, half), BF16),
            pltpu.VMEM(grid + (own, half), BF16),
            pltpu.VMEM(grid + (2, 128), F32),
            pltpu.VMEM(grid + (own, half), BF16),
            pltpu.VMEM(grid + (own, half), BF16),
            pltpu.VMEM(grid + (2, 128), F32),
            pltpu.VMEM((side - 1, side, own, half), BF16),
            pltpu.VMEM((side - 1, side, own, half), BF16),
            pltpu.VMEM((side - 1, side, 2, 128), F32),
            pltpu.VMEM((side - 1, side, 2, 128), F32),
            pltpu.VMEM((side, own, half), BF16),
            pltpu.VMEM((side, own, half), BF16),
            pltpu.VMEM((side, 2, 128), F32),
            pltpu.VMEM((side, 2, 128), F32),
            pltpu.VMEM((side - 1, own, half), BF16),
            pltpu.VMEM((side - 1, own, half), BF16),
            pltpu.VMEM((side - 1, 2, 128), F32),
            pltpu.VMEM((side - 1, 2, 128), F32),
            dma((copies,)),
            dma((copies,)),
            dma((5,)),
        ],
        compiler_params=pltpu.CompilerParams(
            collective_id=1, has_side_effects=True, vmem_limit_bytes=VMEM_BYTES
        ),
        name="combine",
    )(
        acc_a.reshape(2, side, side, own, half),
        acc_b.reshape(2, side, side, own, half),
        stats.reshape(2, side, side, 2, 128),
        qa,
        qb,
        fresh,
        absorb_value,
    )
    return jnp.transpose(out.reshape(requests, steps, heads, -1), (1, 0, 2, 3))


def solution(mesh):
    placed = (
        P("role", "seq", None),
        P("role", "seq"),
        P(("role", "seq"), None),
        P(("role", "seq"), None),
        P(("role", "seq")),
        P(None, "role", None),
        P(None, "role", "seq", None),
        P(None, "role", "seq", None),
        P("seq", None, None),
        P("seq", None, None),
    )
    return jax.shard_map(
        per_device,
        mesh=mesh,
        in_specs=placed,
        out_specs=P(None, "role", "seq", None),
        check_vma=False,
    )
```

```python
import functools

import jax
import jax.numpy as jnp
from jax import lax
from jax.experimental import pallas as pl
from jax.experimental.pallas import tpu as pltpu
from jax.sharding import PartitionSpec as P

FAR = -1e30
LOG2E = 1.4426950408889634
MESH = pl.DeviceIdType.MESH
F32 = jnp.float32
BF16 = jnp.bfloat16
NT = (((1,), (1,)), ((), ()))

CAP = 4
SPAN = 1024
EDGE = 256
VMEM_BYTES = 56 * 1024 * 1024


def iota(shape, dim):
    return lax.broadcasted_iota(jnp.int32, shape, dim)


def place(side):
    seq = lax.axis_index("seq")
    return lax.div(seq, 2 * side), lax.rem(lax.div(seq, 2), side), lax.rem(seq, 2)


def seq_of(side, y, z, c):
    return (y * side + z) * 2 + c


def turned(value, by, size):
    return lax.rem(value + by, size)


def start_together(devices):
    barrier = pltpu.get_barrier_semaphore()
    for device in devices:
        pl.semaphore_signal(barrier, inc=1, device_id=device, device_id_type=MESH)
    pl.semaphore_wait(barrier, len(devices))


def absorb_queries(nope, key_ref):
    rows = nope.shape[0]
    heads = key_ref.shape[0]
    head = lax.rem(iota((rows, 1), 0), heads)
    total = jnp.zeros((rows, key_ref.shape[2]), F32)
    for h in range(heads):
        part = jnp.dot(nope, key_ref[h], preferred_element_type=F32)
        total = total + jnp.where(head == h, part, 0.0)
    return total.astype(BF16)


def gather_rows(source_ref, wide):
    steps, requests, heads, n = source_ref.shape
    for t in range(steps):
        for r in range(requests):
            begin = (r * steps + t) * heads
            wide[begin : begin + heads, :n] = source_ref[t, r].astype(F32)
    return wide[:, :n].astype(BF16)


def exchange_kernel(
    side,
    n_role,
    nope_ref,
    rope_ref,
    key_ref,
    rows_ref,
    owner_ref,
    request_ref,
    qa_ref,
    qb_ref,
    got_ref,
    tag_ref,
    own_a,
    own_b,
    wide,
    packed,
    tags,
    send_sem,
    recv_sem,
    local_sem,
):
    g = lax.axis_index("role")
    seq = lax.axis_index("seq")
    y, z, c = place(side)
    y_peers = [{"role": g, "seq": seq_of(side, turned(y, d, side), z, c)} for d in range(1, side)]
    z_peers = [{"role": g, "seq": seq_of(side, y, turned(z, d, side), c)} for d in range(1, side)]
    x_peers = [{"role": turned(g, d, n_role), "seq": seq} for d in range(1, n_role)]
    mate = {"role": g, "seq": seq_of(side, y, z, 1 - c)}
    start_together(y_peers + z_peers + x_peers + [mate])

    count = [0]

    def send(src, dst, device):
        k = count[0]
        count[0] += 1
        copy = pltpu.make_async_remote_copy(
            src_ref=src,
            dst_ref=dst,
            send_sem=send_sem.at[k],
            recv_sem=recv_sem.at[k],
            device_id=device,
            device_id_type=MESH,
        )
        copy.start()
        return copy

    q_latent = absorb_queries(gather_rows(nope_ref, wide), key_ref)
    half = own_a.shape[1]
    own_a[...] = q_latent[:, :half]
    own_b[:, : q_latent.shape[1] - half] = q_latent[:, half:]
    own_b[:, q_latent.shape[1] - half :] = gather_rows(rope_ref, wide)

    first_a = [send(own_a, qa_ref.at[c, y, z], peer) for peer in y_peers]
    first_b = [send(own_b, qb_ref.at[c, y, z], peer) for peer in z_peers]
    keep_a = pltpu.make_async_copy(own_a, qa_ref.at[c, y, z], local_sem.at[0])
    keep_b = pltpu.make_async_copy(own_b, qb_ref.at[c, y, z], local_sem.at[1])
    keep_a.start()
    keep_b.start()

    send_count = rows_ref.shape[1]
    devices = n_role * 2 * side * side
    owner = owner_ref[...]
    hits = iota((devices, send_count), 0) == owner
    earlier = iota((send_count, send_count), 0) < iota((send_count, send_count), 1)
    before = jnp.dot(hits.astype(BF16), earlier.astype(BF16), preferred_element_type=F32)
    slot = jnp.sum(jnp.where(hits, before, 0.0), axis=0, keepdims=True).astype(jnp.int32)
    position = owner * CAP + slot
    chosen = (iota((devices * CAP, send_count), 0) == position).astype(BF16)
    room = packed.shape[2]
    for i in range(n_role):
        packed[i] = lax.dot_general(
            rows_ref[...], chosen[i * room : (i + 1) * room], NT, preferred_element_type=F32
        ).astype(BF16)
    marks = jnp.broadcast_to((request_ref[...] + 1).astype(BF16), (8, send_count))
    tag_rows = lax.dot_general(marks, chosen, NT, preferred_element_type=F32)
    for i in range(n_role):
        tags[i] = tag_rows[:, i * room : (i + 1) * room]

    crossing = []
    for d in range(1, n_role):
        there = turned(g, d, n_role)
        crossing.append(send(packed.at[there], got_ref.at[g], x_peers[d - 1]))
        crossing.append(send(tags.at[there], tag_ref.at[g], x_peers[d - 1]))
    keep_rows = pltpu.make_async_copy(packed.at[g], got_ref.at[g], local_sem.at[2])
    keep_tags = pltpu.make_async_copy(tags.at[g], tag_ref.at[g], local_sem.at[3])
    keep_rows.start()
    keep_tags.start()

    keep_a.wait()
    for copy in first_a:
        copy.wait_recv()
    line_a = qa_ref.at[c, :, z]
    second_a = [send(line_a, line_a, peer) for peer in z_peers]
    last = [send(line_a, line_a, mate)]
    keep_b.wait()
    for copy in first_b:
        copy.wait_recv()
    line_b = qb_ref.at[c, y]
    second_b = [send(line_b, line_b, peer) for peer in y_peers]
    last.append(send(line_b, line_b, mate))
    for d in range(1, side):
        second_a[d - 1].wait_recv()
        line = qa_ref.at[c, :, turned(z, side - d, side)]
        last.append(send(line, line, mate))
        second_b[d - 1].wait_recv()
        line = qb_ref.at[c, turned(y, side - d, side)]
        last.append(send(line, line, mate))

    keep_rows.wait()
    keep_tags.wait()
    for copy in crossing + last:
        copy.wait_recv()
    for copy in first_a + first_b + crossing + second_a + second_b + last:
        copy.wait_send()


def attend_kernel(
    scale,
    cache_ref,
    ids_ref,
    got_ref,
    tag_ref,
    qa_ref,
    qb_ref,
    aa_ref,
    ab_ref,
    st_ref,
    keys,
    extra,
    top_s,
    tot_s,
    acc_s,
    sems,
):
    chunks = sems.shape[0]
    rows = cache_ref.shape[1]
    part = rows // chunks
    copies = []
    for i in range(chunks):
        copy = pltpu.make_async_copy(
            cache_ref.at[:, pl.ds(i * part, part)], keys.at[:, pl.ds(i * part, part)], sems.at[i]
        )
        copy.start()
        copies.append(copy)

    sources, per = tag_ref.shape[0], tag_ref.shape[2]
    room = sources * per
    tag = jnp.concatenate([tag_ref[i, 0:1, :] for i in range(sources)], axis=1)
    requests = qa_ref.shape[1] // 16
    kinds = iota((8, room), 0)
    same = jnp.where(kinds == requests, 0.0, (kinds + 1).astype(F32)) == tag
    same = same & (kinds <= requests)
    same_f = same.astype(F32)
    earlier = (iota((room, room), 0) < iota((room, room), 1)).astype(BF16)
    before = jnp.dot(same_f.astype(BF16), earlier, preferred_element_type=F32)
    counts = [jnp.sum(same_f[b]).astype(jnp.int32) for b in range(requests)]
    starts = [jnp.int32(0)]
    for b in range(requests):
        starts.append(starts[-1] + counts[b])
    offset = jnp.zeros((8, room), F32)
    for b in range(requests + 1):
        offset = jnp.where(kinds == b, starts[b].astype(F32), offset)
    rank = jnp.sum(jnp.where(same, before + offset, 0.0), axis=0, keepdims=True).astype(jnp.int32)
    moved = (iota((room, room), 0) == rank).astype(BF16)
    flat = jnp.concatenate([got_ref[i] for i in range(sources)], axis=1)
    extra[...] = lax.dot_general(flat, moved, NT, preferred_element_type=F32).astype(BF16)

    ids = ids_ref[...]
    edges = [jnp.int32(0)]
    for b in range(1, requests):
        edges.append(jnp.sum((ids < b).astype(jnp.int32)))
    edges.append(jnp.int32(rows))

    for copy in copies:
        copy.wait()

    count = top_s.shape[0]
    half_q = count // 2
    width_a = qa_ref.shape[2]
    factor = scale * LOG2E
    latent = acc_s.shape[1]
    units = qa_ref.shape[0]
    lane = iota((count, 128), 1)
    row = lax.rem(iota((count, 128), 0), 16)
    top_rows = jnp.zeros((units, 128), F32)
    tot_rows = jnp.zeros((units, 128), F32)

    for b in range(requests):
        top_s[...] = jnp.full(top_s.shape, FAR, F32)
        tot_s[...] = jnp.zeros(tot_s.shape, F32)
        acc_s[...] = jnp.zeros(acc_s.shape, F32)

        def visit(key_block, lower, upper, width, masked):
            columns = iota((1, width), 1)
            inside = (columns >= lower) & (columns < upper)
            for t in range(2):
                here = pl.ds(t * half_q, half_q)
                q_here = pl.ds(t * (units // 2), units // 2)
                qa = qa_ref[q_here, b * 16 : (b + 1) * 16, :].reshape(half_q, width_a)
                qb = qb_ref[q_here, b * 16 : (b + 1) * 16, :].reshape(half_q, qb_ref.shape[2])
                score = jnp.dot(qa, key_block[:width_a], preferred_element_type=F32)
                score += jnp.dot(qb, key_block[width_a:], preferred_element_type=F32)
                score = score * factor
                if masked:
                    score = jnp.where(inside, score, FAR)
                old = top_s[here]
                top = jnp.maximum(old, jnp.max(score, axis=1, keepdims=True))
                expo = jnp.exp2(score - top)
                keep = jnp.exp2(old - top)
                top_s[here] = top
                tot_s[here] = tot_s[here] * keep + jnp.sum(expo, axis=1, keepdims=True)
                acc_s[here] = acc_s[here] * keep + lax.dot_general(
                    expo.astype(BF16), key_block[:latent], NT, preferred_element_type=F32
                )

        def over(source, first, last, lower, upper, width, masked):
            def body(i, _):
                begin = pl.multiple_of(i * width, width)
                block = source[:, pl.ds(begin, width)]
                visit(block, lower - begin, upper - begin, width, masked)
                return 0

            lax.fori_loop(first, last, body, 0)

        lower, upper = edges[b], edges[b + 1]
        span_low = lax.div(lower + (SPAN - 1), SPAN)
        span_high = jnp.maximum(lax.div(upper, SPAN), span_low)
        per_span = SPAN // EDGE
        edge_low, edge_high = lax.div(lower, EDGE), lax.div(upper + (EDGE - 1), EDGE)
        over(keys, span_low, span_high, lower, upper, SPAN, False)
        over(keys, edge_low, jnp.minimum(span_low * per_span, edge_high), lower, upper, EDGE, True)
        over(keys, span_high * per_span, edge_high, lower, upper, EDGE, True)
        over(
            extra,
            lax.div(starts[b], EDGE),
            lax.div(starts[b + 1] + (EDGE - 1), EDGE),
            starts[b],
            starts[b + 1],
            EDGE,
            True,
        )

        for u in range(units):
            piece = acc_s[u * 16 : (u + 1) * 16, :].astype(BF16)
            aa_ref[u, b * 16 : (b + 1) * 16, :] = piece[:, : latent // 2]
            ab_ref[u, b * 16 : (b + 1) * 16, :] = piece[:, latent // 2 :]
        mine = lane == row + b * 16
        top_rows += jnp.sum(jnp.where(mine, top_s[...], 0.0).reshape(units, 16, 128), axis=1)
        tot_rows += jnp.sum(jnp.where(mine, tot_s[...], 0.0).reshape(units, 16, 128), axis=1)
    st_ref[:, 0, :] = top_rows
    st_ref[:, 1, :] = tot_rows


def blend(tops):
    top = functools.reduce(jnp.maximum, tops)
    return top, [jnp.exp2(item - top) for item in tops]


def columns_of(weight, rows):
    n = weight.shape[0]
    pick = iota((n, rows, 128), 2) == iota((n, rows, 128), 1)
    return jnp.sum(jnp.where(pick, weight[:, None, :], 0.0), axis=2, keepdims=True)


def total_of(tots, weights):
    return functools.reduce(jnp.add, [t * w for t, w in zip(tots, weights)])


def acc_of(accs, columns):
    return functools.reduce(jnp.add, [a.astype(F32) * col for a, col in zip(accs, columns)])


def combine_kernel(
    side,
    scale,
    aa_ref,
    ab_ref,
    st_ref,
    qa_ref,
    qb_ref,
    new_ref,
    value_ref,
    out_ref,
    fresh_rows,
    own_a,
    own_b,
    mine_a,
    mine_b,
    mine_st,
    pair_a,
    pair_b,
    pair_st,
    mid_a,
    mid_b,
    mid_st,
    in1_a,
    in1_b,
    in1_sa,
    in1_sb,
    mid2_a,
    mid2_b,
    mid2_sa,
    mid2_sb,
    in2_a,
    in2_b,
    in2_sa,
    in2_sb,
    send_sem,
    recv_sem,
    local_sem,
):
    g = lax.axis_index("role")
    y, z, c = place(side)
    y_peers = [{"role": g, "seq": seq_of(side, turned(y, d, side), z, c)} for d in range(1, side)]
    z_peers = [{"role": g, "seq": seq_of(side, y, turned(z, d, side), c)} for d in range(1, side)]
    mate = {"role": g, "seq": seq_of(side, y, z, 1 - c)}

    keep = [
        pltpu.make_async_copy(aa_ref.at[c], mine_a, local_sem.at[0]),
        pltpu.make_async_copy(ab_ref.at[c], mine_b, local_sem.at[1]),
        pltpu.make_async_copy(st_ref.at[c], mine_st, local_sem.at[2]),
        pltpu.make_async_copy(qa_ref.at[c, y, z], own_a, local_sem.at[3]),
        pltpu.make_async_copy(qb_ref.at[c, y, z], own_b, local_sem.at[4]),
    ]
    for copy in keep:
        copy.start()
    start_together(y_peers + z_peers + [mate])

    count = [0]

    def send(src, dst, device):
        k = count[0]
        count[0] += 1
        copy = pltpu.make_async_remote_copy(
            src_ref=src,
            dst_ref=dst,
            send_sem=send_sem.at[k],
            recv_sem=recv_sem.at[k],
            device_id=device,
            device_id_type=MESH,
        )
        copy.start()
        return copy

    across = [
        send(aa_ref.at[1 - c], pair_a, mate),
        send(ab_ref.at[1 - c], pair_b, mate),
        send(st_ref.at[1 - c], pair_st, mate),
    ]
    for copy in keep:
        copy.wait()

    half = own_a.shape[1]
    rows = own_a.shape[0]
    latent = value_ref.shape[1]
    requests, steps, width = new_ref.shape
    for b in range(requests):
        fresh_rows[b * steps : (b + 1) * steps, :] = new_ref[b].astype(F32)
    new = fresh_rows[...].astype(BF16)
    score = lax.dot_general(own_a[...], new[:, :half], NT, preferred_element_type=F32)
    score += lax.dot_general(own_b[...], new[:, half:], NT, preferred_element_type=F32)
    score = score * (scale * LOG2E)
    fresh = new.shape[0]
    heads = value_ref.shape[0]
    r_row, r_col = iota((rows, fresh), 0), iota((rows, fresh), 1)
    seen = (lax.div(r_row, 16) == lax.div(r_col, steps)) & (
        lax.div(lax.rem(r_row, 16), heads) >= lax.rem(r_col, steps)
    )
    top0 = jnp.max(jnp.where(seen, score, FAR), axis=1, keepdims=True)
    expo = jnp.where(seen, jnp.exp2(score - top0), 0.0)
    tot0 = jnp.sum(expo, axis=1, keepdims=True)
    acc0 = jnp.dot(expo.astype(BF16), new[:, :latent], preferred_element_type=F32)

    for copy in across:
        copy.wait_recv()
    for i in range(side):
        top, weights = blend([mine_st[i, :, 0, :], pair_st[i, :, 0, :]])
        columns = [columns_of(w, rows) for w in weights]
        mid_st[i, :, 0, :] = top
        mid_st[i, :, 1, :] = total_of([mine_st[i, :, 1, :], pair_st[i, :, 1, :]], weights)
        mid_a[i] = acc_of([mine_a[i], pair_a[i]], columns).astype(BF16)
        mid_b[i] = acc_of([mine_b[i], pair_b[i]], columns).astype(BF16)

    over_a, over_b = [], []
    for d in range(1, side):
        there_y, there_z = turned(y, d, side), turned(z, d, side)
        over_a.append(send(mid_a.at[there_y], in1_a.at[d - 1], y_peers[d - 1]))
        over_a.append(send(mid_st.at[there_y], in1_sa.at[d - 1], y_peers[d - 1]))
        over_b.append(send(mid_b.at[:, there_z], in1_b.at[d - 1], z_peers[d - 1]))
        over_b.append(send(mid_st.at[:, there_z], in1_sb.at[d - 1], z_peers[d - 1]))

    def settle(copies, mine_acc, mine_stat, in_acc, in_stat):
        for copy in copies:
            copy.wait_recv()
        stats = [mine_stat] + [in_stat[d] for d in range(side - 1)]
        top, weights = blend([s[:, 0, :] for s in stats])
        columns = [columns_of(w, rows) for w in weights]
        total = total_of([s[:, 1, :] for s in stats], weights)
        acc = acc_of([mine_acc] + [in_acc[d] for d in range(side - 1)], columns)
        return top, total, acc

    top, total, acc = settle(over_a, mid_a[y], mid_st[y], in1_a, in1_sa)
    mid2_sa[:, 0, :] = top
    mid2_sa[:, 1, :] = total
    mid2_a[...] = acc.astype(BF16)
    next_a = []
    for d in range(1, side):
        there = turned(z, d, side)
        next_a.append(send(mid2_a.at[there], in2_a.at[d - 1], z_peers[d - 1]))
        next_a.append(send(mid2_sa.at[there], in2_sa.at[d - 1], z_peers[d - 1]))
    top, total, acc = settle(over_b, mid_b[:, z], mid_st[:, z], in1_b, in1_sb)
    mid2_sb[:, 0, :] = top
    mid2_sb[:, 1, :] = total
    mid2_b[...] = acc.astype(BF16)
    next_b = []
    for d in range(1, side):
        there = turned(y, d, side)
        next_b.append(send(mid2_b.at[there], in2_b.at[d - 1], y_peers[d - 1]))
        next_b.append(send(mid2_sb.at[there], in2_sb.at[d - 1], y_peers[d - 1]))

    def finish(copies, mine_acc, mine_stat, in_acc, in_stat, fresh_acc):
        for copy in copies:
            copy.wait_recv()
        stats = [mine_stat] + [in_stat[d] for d in range(side - 1)]
        top, weights = blend([s[0:1, :] for s in stats])
        columns = [columns_of(w, rows)[0] for w in weights]
        total = total_of([s[1:2, :] for s in stats], weights)
        acc = acc_of([mine_acc] + [in_acc[d] for d in range(side - 1)], columns)
        top_c, tot_c = columns_of(top, rows)[0], columns_of(total, rows)[0]
        best = jnp.maximum(top_c, top0)
        keep_c, keep_0 = jnp.exp2(top_c - best), jnp.exp2(top0 - best)
        tot = tot_c * keep_c + tot0 * keep_0
        return ((acc * keep_c + fresh_acc * keep_0) / tot).astype(BF16)

    out_a = finish(next_a, mid2_a[z], mid2_sa[z], in2_a, in2_sa, acc0[:, : latent // 2])
    out_b = finish(next_b, mid2_b[y], mid2_sb[y], in2_b, in2_sb, acc0[:, latent // 2 :])
    head = lax.rem(iota((rows, 1), 0), heads)
    result = jnp.zeros((rows, value_ref.shape[2]), F32)
    for h in range(heads):
        part = jnp.dot(out_a, value_ref[h, : latent // 2], preferred_element_type=F32)
        part += jnp.dot(out_b, value_ref[h, latent // 2 :], preferred_element_type=F32)
        result = result + jnp.where(head == h, part, 0.0)
    for t in range(steps):
        for b in range(requests):
            begin = (b * steps + t) * heads
            out_ref[t, b] = result[begin : begin + heads].astype(BF16)

    for copy in across + over_a + over_b + next_a + next_b:
        copy.wait_send()


def per_device(
    cache_rows,
    cache_request,
    sent_rows,
    sent_owner,
    sent_request,
    new_rows,
    query_nope,
    query_rope,
    absorb_key,
    absorb_value,
):
    n_role = lax.axis_size("role")
    n_seq = lax.axis_size("seq")
    side = 1
    while 2 * side * side < n_seq:
        side += 1
    steps, requests, heads, nope = query_nope.shape
    rope = query_rope.shape[3]
    latent = absorb_key.shape[2]
    width = sent_rows.shape[1]
    half = latent // 2
    own = steps * requests * heads
    send = sent_rows.shape[0]
    room = CAP * n_seq
    scale = 1.0 / float(nope + rope) ** 0.5
    local_rows = cache_rows.shape[1]

    cache_columns = cache_rows[0].T
    fresh = jnp.transpose(new_rows, (1, 0, 2))

    vmem = pl.BlockSpec(memory_space=pltpu.VMEM)
    hbm = pl.BlockSpec(memory_space=pl.ANY)
    dma = pltpu.SemaphoreType.DMA

    copies = 4 * (side - 1) + 2 * (n_role - 1) + 2 * side
    qa, qb, got, tags = pl.pallas_call(
        functools.partial(exchange_kernel, side, n_role),
        out_shape=(
            jax.ShapeDtypeStruct((2, side, side, own, half), BF16),
            jax.ShapeDtypeStruct((2, side, side, own, width - half), BF16),
            jax.ShapeDtypeStruct((n_role, width, room), BF16),
            jax.ShapeDtypeStruct((n_role, 8, room), F32),
        ),
        in_specs=[vmem] * 6,
        out_specs=(hbm, hbm, hbm, hbm),
        scratch_shapes=[
            pltpu.VMEM((own, half), BF16),
            pltpu.VMEM((own, width - half), BF16),
            pltpu.VMEM((own, nope), F32),
            pltpu.VMEM((n_role, width, room), BF16),
            pltpu.VMEM((n_role, 8, room), F32),
            dma((copies,)),
            dma((copies,)),
            dma((4,)),
        ],
        compiler_params=pltpu.CompilerParams(
            collective_id=0, has_side_effects=True, vmem_limit_bytes=VMEM_BYTES
        ),
        name="exchange",
    )(
        query_nope,
        query_rope,
        absorb_key,
        sent_rows.T,
        sent_owner.reshape(1, send),
        sent_request.reshape(1, send),
    )

    units = 2 * side * side
    count = units * steps * heads
    acc_a, acc_b, stats = pl.pallas_call(
        functools.partial(attend_kernel, scale),
        out_shape=(
            jax.ShapeDtypeStruct((units, own, half), BF16),
            jax.ShapeDtypeStruct((units, own, half), BF16),
            jax.ShapeDtypeStruct((units, 2, 128), F32),
        ),
        in_specs=[hbm, vmem, vmem, vmem, vmem, vmem],
        out_specs=(vmem, vmem, vmem),
        scratch_shapes=[
            pltpu.VMEM((width, local_rows), BF16),
            pltpu.VMEM((width, n_role * room), BF16),
            pltpu.VMEM((count, 1), F32),
            pltpu.VMEM((count, 1), F32),
            pltpu.VMEM((count, latent), F32),
            dma((4,)),
        ],
        compiler_params=pltpu.CompilerParams(vmem_limit_bytes=VMEM_BYTES),
        name="attend",
    )(
        cache_columns,
        cache_request,
        got,
        tags,
        qa.reshape(units, own, half),
        qb.reshape(units, own, width - half),
    )

    grid = (side, side)
    copies = 3 + 8 * (side - 1)
    out = pl.pallas_call(
        functools.partial(combine_kernel, side, scale),
        out_shape=jax.ShapeDtypeStruct((steps, requests, heads, absorb_value.shape[2]), BF16),
        in_specs=[hbm] * 5 + [vmem] * 2,
        out_specs=vmem,
        scratch_shapes=[
            pltpu.VMEM((steps * requests, width), F32),
            pltpu.VMEM((own, half), BF16),
            pltpu.VMEM((own, width - half), BF16),
            pltpu.VMEM(grid + (own, half), BF16),
            pltpu.VMEM(grid + (own, half), BF16),
            pltpu.VMEM(grid + (2, 128), F32),
            pltpu.VMEM(grid + (own, half), BF16),
            pltpu.VMEM(grid + (own, half), BF16),
            pltpu.VMEM(grid + (2, 128), F32),
            pltpu.VMEM(grid + (own, half), BF16),
            pltpu.VMEM(grid + (own, half), BF16),
            pltpu.VMEM(grid + (2, 128), F32),
            pltpu.VMEM((side - 1, side, own, half), BF16),
            pltpu.VMEM((side - 1, side, own, half), BF16),
            pltpu.VMEM((side - 1, side, 2, 128), F32),
            pltpu.VMEM((side - 1, side, 2, 128), F32),
            pltpu.VMEM((side, own, half), BF16),
            pltpu.VMEM((side, own, half), BF16),
            pltpu.VMEM((side, 2, 128), F32),
            pltpu.VMEM((side, 2, 128), F32),
            pltpu.VMEM((side - 1, own, half), BF16),
            pltpu.VMEM((side - 1, own, half), BF16),
            pltpu.VMEM((side - 1, 2, 128), F32),
            pltpu.VMEM((side - 1, 2, 128), F32),
            dma((copies,)),
            dma((copies,)),
            dma((5,)),
        ],
        compiler_params=pltpu.CompilerParams(
            collective_id=1, has_side_effects=True, vmem_limit_bytes=VMEM_BYTES
        ),
        name="combine",
    )(
        acc_a.reshape(2, side, side, own, half),
        acc_b.reshape(2, side, side, own, half),
        stats.reshape(2, side, side, 2, 128),
        qa,
        qb,
        fresh,
        absorb_value,
    )
    return out


def solution(mesh):
    placed = (
        P("role", "seq", None),
        P("role", "seq"),
        P(("role", "seq"), None),
        P(("role", "seq"), None),
        P(("role", "seq")),
        P(None, "role", None),
        P(None, "role", "seq", None),
        P(None, "role", "seq", None),
        P("seq", None, None),
        P("seq", None, None),
    )
    return jax.shard_map(
        per_device,
        mesh=mesh,
        in_specs=placed,
        out_specs=P(None, "role", "seq", None),
        check_vma=False,
    )
```

```python
import functools

import jax
import jax.numpy as jnp
from jax import lax
from jax.experimental import pallas as pl
from jax.experimental.pallas import tpu as pltpu
from jax.sharding import PartitionSpec as P

FAR = -1e30
LOG2E = 1.4426950408889634
MESH = pl.DeviceIdType.MESH
F32 = jnp.float32
BF16 = jnp.bfloat16
NT = (((1,), (1,)), ((), ()))

CAP = 4
SPAN = 512
ROWS = 16
VMEM_BYTES = 56 * 1024 * 1024


def iota(shape, dim):
    return lax.broadcasted_iota(jnp.int32, shape, dim)


def place(side):
    seq = lax.axis_index("seq")
    return lax.div(seq, 2 * side), lax.rem(lax.div(seq, 2), side), lax.rem(seq, 2)


def seq_of(side, y, z, c):
    return (y * side + z) * 2 + c


def turned(value, by, size):
    return lax.rem(value + by, size)


def absorb_queries(nope, key_ref):
    rows = nope.shape[0]
    heads = key_ref.shape[0]
    head = lax.rem(iota((rows, 1), 0), heads)
    total = jnp.zeros((rows, key_ref.shape[2]), F32)
    for h in range(heads):
        part = jnp.dot(nope, key_ref[h], preferred_element_type=F32)
        total = total + jnp.where(head == h, part, 0.0)
    return total.astype(BF16)


def gather_rows(source_ref, wide):
    steps, requests, heads, n = source_ref.shape
    for t in range(steps):
        for r in range(requests):
            begin = (r * steps + t) * heads
            wide[begin : begin + heads, :n] = source_ref[t, r].astype(F32)
    return wide[:, :n].astype(BF16)


def pick(index, values):
    result = values[-1]
    for b in reversed(range(len(values) - 1)):
        result = jnp.where(index == b, values[b], result)
    return result


def plan_steps(edges, rows):
    requests = len(edges) - 1
    first, steps = [], []
    for b in range(requests):
        begin = lax.div(edges[b], SPAN)
        end = lax.div(edges[b + 1] + (SPAN - 1), SPAN)
        first.append(begin)
        steps.append(jnp.where(edges[b + 1] > edges[b], end - begin, 0))
    offset = [jnp.int32(0)]
    for b in range(requests):
        offset.append(offset[-1] + steps[b])
    lasts = [(steps[b] > 0, jnp.where(steps[b] > 0, offset[b + 1] - 1, 0)) for b in range(requests)]
    entries = []
    for j in range(rows // SPAN + requests - 1):
        request = jnp.int32(0)
        for b in range(1, requests):
            request += (j >= offset[b]).astype(jnp.int32)
        base = pick(request, offset[:-1])
        live = j < offset[-1]
        block = jnp.where(live, pick(request, first) + (j - base), 0)
        begin = block * SPAN
        lower = pick(request, edges[:-1])
        upper = jnp.where(live, pick(request, edges[1:]), 0)
        entries.append((request, block, lower - begin, upper - begin, j == base))
    return entries, lasts


def score_steps(entries, lasts, keys, extra, queries, s_ref, e_ref, m_ref, top_ref):
    requests, _, width = queries.shape
    columns = iota((1, SPAN), 1)
    for j, (request, block, lower, upper, fresh) in enumerate(entries):
        score = jnp.dot(queries[request], keys[block], preferred_element_type=F32)
        score = jnp.where((columns >= lower) & (columns < upper), score, FAR)
        s_ref[j] = score
        top = jnp.max(score, axis=1, keepdims=True)
        m_ref[j] = jnp.where(fresh, top, jnp.maximum(top, m_ref[j - 1])) if j else top
    tag = extra[width : width + 1, :].astype(F32)
    for b in range(requests):
        score = jnp.dot(queries[b], extra[:width, :], preferred_element_type=F32)
        score = jnp.where(tag == b + 1.0, score, FAR)
        e_ref[b] = score
        some, last = lasts[b]
        top = jnp.max(score, axis=1, keepdims=True)
        top_ref[b] = jnp.maximum(top, jnp.where(some, m_ref[last], FAR))


def value_steps(entries, lasts, factor, latent, keys, extra, s_ref, e_ref, top_ref, l_ref, h_ref):
    requests = len(lasts)
    for j, (request, block, _, _, fresh) in enumerate(entries):
        expo = jnp.exp2(s_ref[j] * factor - top_ref[request] * factor)
        total = jnp.sum(expo, axis=1, keepdims=True)
        part = lax.dot_general(
            expo.astype(BF16), keys[block, :latent], NT, preferred_element_type=F32
        )
        if j:
            keep = jnp.where(fresh, 0.0, 1.0)
            total += l_ref[j - 1] * keep
            part += h_ref[j - 1] * keep
        l_ref[j] = total
        h_ref[j] = part
    sums = []
    for b, (some, last) in enumerate(lasts):
        expo = jnp.exp2(e_ref[b] * factor - top_ref[b] * factor)
        keep = jnp.where(some, 1.0, 0.0)
        total = jnp.sum(expo, axis=1, keepdims=True) + l_ref[last] * keep
        part = lax.dot_general(
            expo.astype(BF16), extra[:latent, :], NT, preferred_element_type=F32
        )
        sums.append((total, part + h_ref[last] * keep))
    return sums


def write_parts(sums, factor, side, top_ref, a_ref, b_ref, st_ref):
    units = side * side
    count, latent = sums[0][1].shape
    lane = iota((count, 128), 1)
    row = lax.rem(iota((count, 128), 0), ROWS)
    tops = jnp.zeros((units, 128), F32)
    tots = jnp.zeros((units, 128), F32)
    for b, (total, whole) in enumerate(sums):
        for u in range(units):
            piece = whole[u * ROWS : (u + 1) * ROWS].astype(BF16)
            dy, dz = u // side, u % side
            a_ref[dy, dz, b * ROWS : (b + 1) * ROWS, :] = piece[:, : latent // 2]
            b_ref[dz, dy, b * ROWS : (b + 1) * ROWS, :] = piece[:, latent // 2 :]
        mine = lane == row + b * ROWS
        tops += jnp.sum(
            jnp.where(mine, top_ref[b] * factor, 0.0).reshape(units, ROWS, 128), axis=1
        )
        tots += jnp.sum(jnp.where(mine, total, 0.0).reshape(units, ROWS, 128), axis=1)
    for u in range(units):
        st_ref[u // side, u % side, 0:1, :] = tops[u : u + 1]
        st_ref[u // side, u % side, 1:2, :] = tots[u : u + 1]


def line_up(side, a_ref, b_ref, queries):
    half = a_ref.shape[3]
    for b in range(queries.shape[0]):
        for u in range(side * side):
            dy, dz = u // side, u % side
            here = slice(u * ROWS, (u + 1) * ROWS)
            queries[b, here, :half] = a_ref[dz, dy, b * ROWS : (b + 1) * ROWS, :]
            queries[b, here, half:] = b_ref[dy, dz, b * ROWS : (b + 1) * ROWS, :]


def blend(tops):
    top = functools.reduce(jnp.maximum, tops)
    return top, [jnp.exp2(item - top) for item in tops]


def columns_of(weight, rows):
    n = weight.shape[0]
    chosen = iota((n, rows, 128), 2) == iota((n, rows, 128), 1)
    return jnp.sum(jnp.where(chosen, weight[:, None, :], 0.0), axis=2, keepdims=True)


def total_of(tots, weights):
    return functools.reduce(jnp.add, [t * w for t, w in zip(tots, weights)])


def acc_of(accs, columns):
    return functools.reduce(jnp.add, [a.astype(F32) * col for a, col in zip(accs, columns)])


def fused_kernel(
    side,
    n_role,
    scale,
    cache_ref,
    ids_ref,
    rows_ref,
    owner_ref,
    request_ref,
    new_ref,
    nope_ref,
    rope_ref,
    key_ref,
    value_ref,
    out_ref,
    keys,
    key_s,
    value_s,
    rows_s,
    wide,
    fresh_rows,
    packed,
    got,
    extra,
    buf_a,
    buf_b,
    mate_a,
    mate_b,
    queries,
    mate_queries,
    s_own,
    s_mate,
    e_own,
    e_mate,
    top_own,
    top_mate,
    m_ref,
    l_ref,
    h_ref,
    mine_a,
    mine_b,
    mine_st,
    give_a,
    give_b,
    give_st,
    pair_a,
    pair_b,
    pair_st,
    in1_a,
    in1_b,
    in1_sa,
    in1_sb,
    mid2_a,
    mid2_b,
    mid2_sa,
    mid2_sb,
    in2_a,
    in2_b,
    in2_sa,
    in2_sb,
    send_sem,
    recv_sem,
    local_sem,
):
    g = lax.axis_index("role")
    seq = lax.axis_index("seq")
    y, z, c = place(side)
    others = range(1, side)
    y_peers = [{"role": g, "seq": seq_of(side, turned(y, d, side), z, c)} for d in others]
    z_peers = [{"role": g, "seq": seq_of(side, y, turned(z, d, side), c)} for d in others]
    x_peers = [{"role": turned(g, d, n_role), "seq": seq} for d in range(1, n_role)]
    mate = {"role": g, "seq": seq_of(side, y, z, 1 - c)}
    peers = y_peers + z_peers + x_peers + [mate]

    barrier = pltpu.get_barrier_semaphore()
    for device in peers:
        pl.semaphore_signal(barrier, inc=1, device_id=device, device_id_type=MESH)

    width, rows = cache_ref.shape
    local = []

    def fetch(src, dst):
        copy = pltpu.make_async_copy(src, dst, local_sem.at[len(local)])
        copy.start()
        local.append(copy)
        return copy

    key_copy = fetch(key_ref, key_s)
    rows_copy = fetch(rows_ref, rows_s)
    cache_copies = [
        fetch(cache_ref.at[:, pl.ds(i * SPAN, SPAN)], keys.at[i]) for i in range(rows // SPAN)
    ]
    value_copy = fetch(value_ref, value_s)

    count = [0]
    started = []

    def send(src, dst, device):
        k = count[0]
        count[0] += 1
        copy = pltpu.make_async_remote_copy(
            src_ref=src,
            dst_ref=dst,
            send_sem=send_sem.at[k],
            recv_sem=recv_sem.at[k],
            device_id=device,
            device_id_type=MESH,
        )
        copy.start()
        started.append(copy)
        return copy

    half = buf_a.shape[3]
    latent = key_ref.shape[2]
    x_nope = gather_rows(nope_ref, wide)
    key_copy.wait()
    q_latent = absorb_queries(x_nope, key_s)
    buf_a[0, 0] = q_latent[:, :half]
    buf_b[0, 0, :, : latent - half] = q_latent[:, half:]
    buf_b[0, 0, :, latent - half :] = gather_rows(rope_ref, wide)

    pl.semaphore_wait(barrier, len(peers))

    first_a = [send(buf_a.at[0, 0], buf_a.at[0, side - d], y_peers[d - 1]) for d in others]
    first_b = [send(buf_b.at[0, 0], buf_b.at[0, side - d], z_peers[d - 1]) for d in others]
    own_a = [send(buf_a.at[0, 0], buf_a.at[side - d, 0], z_peers[d - 1]) for d in others]
    own_b = [send(buf_b.at[0, 0], buf_b.at[side - d, 0], y_peers[d - 1]) for d in others]

    send_count = rows_ref.shape[1]
    devices = n_role * 2 * side * side
    owner = owner_ref[...]
    hits = iota((devices, send_count), 0) == owner
    earlier = iota((send_count, send_count), 0) < iota((send_count, send_count), 1)
    before = jnp.dot(hits.astype(BF16), earlier.astype(BF16), preferred_element_type=F32)
    slot = jnp.sum(jnp.where(hits, before, 0.0), axis=0, keepdims=True).astype(jnp.int32)
    position = owner * CAP + slot
    chosen = (iota((devices * CAP, send_count), 0) == position).astype(BF16)
    room = packed.shape[2]
    marked = jnp.broadcast_to((request_ref[...] + 1).astype(BF16), (ROWS, send_count))
    rows_copy.wait()

    for i in range(n_role):
        part = chosen[i * room : (i + 1) * room]
        packed[i, :width] = lax.dot_general(
            rows_s[...], part, NT, preferred_element_type=F32
        ).astype(BF16)
        packed[i, width:] = lax.dot_general(
            marked, part, NT, preferred_element_type=F32
        ).astype(BF16)
    crossing = [
        send(packed.at[turned(g, d, n_role)], got.at[n_role - d - 1], x_peers[d - 1])
        for d in range(1, n_role)
    ]
    extra[:, :room] = packed[g]

    for copy in first_a:
        copy.wait_recv()
    second_a = [
        send(buf_a.at[0, pl.ds(1, side - 1)], buf_a.at[side - d, pl.ds(1, side - 1)], z_peers[d - 1])
        for d in others
    ]
    across = [send(buf_a.at[0], mate_a.at[0], mate)]
    for copy in first_b:
        copy.wait_recv()
    second_b = [
        send(buf_b.at[0, pl.ds(1, side - 1)], buf_b.at[side - d, pl.ds(1, side - 1)], y_peers[d - 1])
        for d in others
    ]
    across.append(send(buf_b.at[0], mate_b.at[0], mate))

    own_rows = buf_a.shape[2]
    requests, steps, _ = new_ref.shape
    heads = key_ref.shape[0]
    factor = scale * LOG2E
    for b in range(requests):
        fresh_rows[b * steps : (b + 1) * steps, :] = new_ref[b].astype(F32)
    new = fresh_rows[...].astype(BF16)
    score = lax.dot_general(buf_a[0, 0], new[:, :half], NT, preferred_element_type=F32)
    score += lax.dot_general(buf_b[0, 0], new[:, half:], NT, preferred_element_type=F32)
    score = score * factor
    r_row, r_col = iota(score.shape, 0), iota(score.shape, 1)
    seen = (lax.div(r_row, ROWS) == lax.div(r_col, steps)) & (
        lax.div(lax.rem(r_row, ROWS), heads) >= lax.rem(r_col, steps)
    )
    top0 = jnp.max(jnp.where(seen, score, FAR), axis=1, keepdims=True)
    expo = jnp.where(seen, jnp.exp2(score - top0), 0.0)
    tot0 = jnp.sum(expo, axis=1, keepdims=True)
    acc0 = jnp.dot(expo.astype(BF16), new[:, :latent], preferred_element_type=F32)

    ids = ids_ref[...]
    edges = [jnp.int32(0)]
    for b in range(1, requests):
        edges.append(jnp.sum((ids < b).astype(jnp.int32)))
    edges.append(jnp.int32(rows))

    entries, lasts = plan_steps(edges, rows)

    for copy in own_a + second_a:
        copy.wait_recv()
    across.append(send(buf_a.at[pl.ds(1, side - 1)], mate_a.at[pl.ds(1, side - 1)], mate))
    for copy in own_b + second_b:
        copy.wait_recv()
    across.append(send(buf_b.at[pl.ds(1, side - 1)], mate_b.at[pl.ds(1, side - 1)], mate))
    for copy in cache_copies:
        copy.wait()

    line_up(side, buf_a, buf_b, queries)
    for copy in crossing:
        copy.wait_recv()
    for i in range(1, n_role):
        extra[:, i * room : (i + 1) * room] = got[i - 1]
    score_steps(entries, lasts, keys, extra, queries, s_own, e_own, m_ref, top_own)
    for copy in across:
        copy.wait_recv()
    line_up(side, mate_a, mate_b, mate_queries)
    score_steps(entries, lasts, keys, extra, mate_queries, s_mate, e_mate, m_ref, top_mate)
    sums = value_steps(
        entries, lasts, factor, latent, keys, extra, s_mate, e_mate, top_mate, l_ref, h_ref
    )
    write_parts(sums, factor, side, top_mate, give_a, give_b, give_st)
    halves = [
        send(give_a, pair_a, mate),
        send(give_b, pair_b, mate),
        send(give_st, pair_st, mate),
    ]
    sums = value_steps(
        entries, lasts, factor, latent, keys, extra, s_own, e_own, top_own, l_ref, h_ref
    )
    write_parts(sums, factor, side, top_own, mine_a, mine_b, mine_st)
    for copy in halves:
        copy.wait_recv()

    for i in range(side):
        top, weights = blend([mine_st[i, :, 0, :], pair_st[i, :, 0, :]])
        columns = [columns_of(w, own_rows) for w in weights]
        total = total_of([mine_st[i, :, 1, :], pair_st[i, :, 1, :]], weights)
        mine_st[i, :, 0, :] = top
        mine_st[i, :, 1, :] = total
        mine_a[i] = acc_of([mine_a[i], pair_a[i]], columns).astype(BF16)
        for k in range(side):
            mine_b[k, i] = acc_of(
                [mine_b[k, i], pair_b[k, i]], [col[k] for col in columns]
            ).astype(BF16)

    over_a, over_b = [], []
    for d in others:
        over_a.append(send(mine_a.at[d], in1_a.at[d - 1], y_peers[d - 1]))
        over_b.append(send(mine_b.at[d], in1_b.at[d - 1], z_peers[d - 1]))
        over_a.append(send(mine_st.at[d], in1_sa.at[d - 1], y_peers[d - 1]))
        over_b.append(send(mine_st.at[:, d], in1_sb.at[d - 1], z_peers[d - 1]))

    def settle(copies, mine_acc, mine_stat, in_acc, in_stat):
        for copy in copies:
            copy.wait_recv()
        stats = [mine_stat] + [in_stat[d] for d in range(side - 1)]
        top, weights = blend([s[:, 0, :] for s in stats])
        columns = [columns_of(w, own_rows) for w in weights]
        total = total_of([s[:, 1, :] for s in stats], weights)
        acc = acc_of([mine_acc] + [in_acc[d] for d in range(side - 1)], columns)
        return top, total, acc

    top, total, acc = settle(over_a, mine_a[0], mine_st[0], in1_a, in1_sa)
    mid2_sa[:, 0, :] = top
    mid2_sa[:, 1, :] = total
    mid2_a[...] = acc.astype(BF16)
    next_a, next_b = [], []
    for d in others:
        next_a.append(send(mid2_a.at[d], in2_a.at[d - 1], z_peers[d - 1]))
        next_a.append(send(mid2_sa.at[d], in2_sa.at[d - 1], z_peers[d - 1]))
    top, total, acc = settle(over_b, mine_b[0], mine_st[:, 0], in1_b, in1_sb)
    mid2_sb[:, 0, :] = top
    mid2_sb[:, 1, :] = total
    mid2_b[...] = acc.astype(BF16)
    for d in others:
        next_b.append(send(mid2_b.at[d], in2_b.at[d - 1], y_peers[d - 1]))
        next_b.append(send(mid2_sb.at[d], in2_sb.at[d - 1], y_peers[d - 1]))

    def finish(copies, mine_acc, mine_stat, in_acc, in_stat, fresh_acc):
        for copy in copies:
            copy.wait_recv()
        stats = [mine_stat] + [in_stat[d] for d in range(side - 1)]
        top, weights = blend([s[0:1, :] for s in stats])
        columns = [columns_of(w, own_rows)[0] for w in weights]
        total = total_of([s[1:2, :] for s in stats], weights)
        acc = acc_of([mine_acc] + [in_acc[d] for d in range(side - 1)], columns)
        top_c, tot_c = columns_of(top, own_rows)[0], columns_of(total, own_rows)[0]
        best = jnp.maximum(top_c, top0)
        keep_c, keep_0 = jnp.exp2(top_c - best), jnp.exp2(top0 - best)
        tot = tot_c * keep_c + tot0 * keep_0
        return ((acc * keep_c + fresh_acc * keep_0) / tot).astype(BF16)

    value_copy.wait()
    out_a = finish(next_a, mid2_a[0], mid2_sa[0], in2_a, in2_sa, acc0[:, : latent // 2])
    out_b = finish(next_b, mid2_b[0], mid2_sb[0], in2_b, in2_sb, acc0[:, latent // 2 :])
    head = lax.rem(iota((own_rows, 1), 0), heads)
    result = jnp.zeros((own_rows, value_ref.shape[2]), F32)
    for h in range(heads):
        part = jnp.dot(out_a, value_s[h, : latent // 2], preferred_element_type=F32)
        part += jnp.dot(out_b, value_s[h, latent // 2 :], preferred_element_type=F32)
        result = result + jnp.where(head == h, part, 0.0)
    for t in range(steps):
        for b in range(requests):
            begin = (b * steps + t) * heads
            out_ref[t, b] = result[begin : begin + heads].astype(BF16)

    for copy in started:
        copy.wait_send()


def per_device(
    cache_rows,
    cache_request,
    sent_rows,
    sent_owner,
    sent_request,
    new_rows,
    query_nope,
    query_rope,
    absorb_key,
    absorb_value,
):
    n_role = lax.axis_size("role")
    n_seq = lax.axis_size("seq")
    side = 1
    while 2 * side * side < n_seq:
        side += 1
    steps, requests, heads, nope = query_nope.shape
    rope = query_rope.shape[3]
    latent = absorb_key.shape[2]
    width = sent_rows.shape[1]
    half = latent // 2
    own = steps * requests * heads
    send = sent_rows.shape[0]
    room = CAP * n_seq
    scale = 1.0 / float(nope + rope) ** 0.5
    local_rows = cache_rows.shape[1]
    units = side * side
    count = units * steps * heads
    listed = local_rows // SPAN + requests - 1

    vmem = pl.BlockSpec(memory_space=pltpu.VMEM)
    hbm = pl.BlockSpec(memory_space=pl.ANY)
    dma = pltpu.SemaphoreType.DMA
    grid = (side, side)
    far = side - 1

    def bf16(*shape):
        return pltpu.VMEM(shape, BF16)

    def f32(*shape):
        return pltpu.VMEM(shape, F32)

    copies = 14 * far + (n_role - 1) + 4 + 3
    return pl.pallas_call(
        functools.partial(fused_kernel, side, n_role, scale),
        out_shape=jax.ShapeDtypeStruct((steps, requests, heads, absorb_value.shape[2]), BF16),
        in_specs=[hbm, vmem, hbm, vmem, vmem, vmem, vmem, vmem, hbm, hbm],
        out_specs=vmem,
        scratch_shapes=[
            bf16(local_rows // SPAN, width, SPAN),
            bf16(heads, nope, latent),
            bf16(heads, latent, absorb_value.shape[2]),
            bf16(width, send),
            f32(own, nope),
            f32(steps * requests, width),
            bf16(n_role, width + ROWS, room),
            bf16(n_role - 1, width + ROWS, room),
            bf16(width + ROWS, n_role * room),
            bf16(side, side, own, half),
            bf16(side, side, own, width - half),
            bf16(side, side, own, half),
            bf16(side, side, own, width - half),
            bf16(requests, count, width),
            bf16(requests, count, width),
            f32(listed, count, SPAN),
            f32(listed, count, SPAN),
            f32(requests, count, n_role * room),
            f32(requests, count, n_role * room),
            f32(requests, count, 1),
            f32(requests, count, 1),
            f32(listed, count, 1),
            f32(listed, count, 1),
            f32(listed, count, latent),
            bf16(side, side, own, half),
            bf16(side, side, own, half),
            f32(side, side, 2, 128),
            bf16(side, side, own, half),
            bf16(side, side, own, half),
            f32(side, side, 2, 128),
            bf16(side, side, own, half),
            bf16(side, side, own, half),
            f32(side, side, 2, 128),
            bf16(far, side, own, half),
            bf16(far, side, own, half),
            f32(far, side, 2, 128),
            f32(far, side, 2, 128),
            bf16(side, own, half),
            bf16(side, own, half),
            f32(side, 2, 128),
            f32(side, 2, 128),
            bf16(far, own, half),
            bf16(far, own, half),
            f32(far, 2, 128),
            f32(far, 2, 128),
            dma((copies,)),
            dma((copies,)),
            dma((local_rows // SPAN + 3,)),
        ],
        compiler_params=pltpu.CompilerParams(
            collective_id=0, has_side_effects=True, vmem_limit_bytes=VMEM_BYTES
        ),
        name="fused",
    )(
        cache_rows[0].T,
        cache_request,
        sent_rows.T,
        sent_owner.reshape(1, send),
        sent_request.reshape(1, send),
        jnp.transpose(new_rows, (1, 0, 2)),
        query_nope,
        query_rope,
        absorb_key,
        absorb_value,
    )


def solution(mesh):
    placed = (
        P("role", "seq", None),
        P("role", "seq"),
        P(("role", "seq"), None),
        P(("role", "seq"), None),
        P(("role", "seq")),
        P(None, "role", None),
        P(None, "role", "seq", None),
        P(None, "role", "seq", None),
        P("seq", None, None),
        P("seq", None, None),
    )
    return jax.shard_map(
        per_device,
        mesh=mesh,
        in_specs=placed,
        out_specs=P(None, "role", "seq", None),
        check_vma=False,
    )
```

```python
import functools

import jax
import jax.numpy as jnp
from jax import lax
from jax.experimental import pallas as pl
from jax.experimental.pallas import tpu as pltpu
from jax.sharding import PartitionSpec as P

FAR = -1e30
LOG2E = 1.4426950408889634
MESH = pl.DeviceIdType.MESH
F32 = jnp.float32
BF16 = jnp.bfloat16
NT = (((1,), (1,)), ((), ()))

CAP = 4
SPAN = 512
ROWS = 16
VMEM_BYTES = 56 * 1024 * 1024


def iota(shape, dim):
    return lax.broadcasted_iota(jnp.int32, shape, dim)


def place(side):
    seq = lax.axis_index("seq")
    return lax.div(seq, 2 * side), lax.rem(lax.div(seq, 2), side), lax.rem(seq, 2)


def seq_of(side, y, z, c):
    return (y * side + z) * 2 + c


def turned(value, by, size):
    return lax.rem(value + by, size)


def absorb_queries(nope, key_ref):
    rows = nope.shape[0]
    heads = key_ref.shape[0]
    head = lax.rem(iota((rows, 1), 0), heads)
    total = jnp.zeros((rows, key_ref.shape[2]), F32)
    for h in range(heads):
        part = jnp.dot(nope, key_ref[h], preferred_element_type=F32)
        total = total + jnp.where(head == h, part, 0.0)
    return total.astype(BF16)


def gather_rows(source_ref, wide):
    steps, requests, heads, n = source_ref.shape
    for t in range(steps):
        for r in range(requests):
            begin = (r * steps + t) * heads
            wide[begin : begin + heads, :n] = source_ref[t, r].astype(F32)
    return wide[:, :n].astype(BF16)


def pick(index, values):
    result = values[-1]
    for b in reversed(range(len(values) - 1)):
        result = jnp.where(index == b, values[b], result)
    return result


def folded(combine, wide):
    return functools.reduce(combine, [wide[:, i : i + 128] for i in range(0, wide.shape[1], 128)])


def plan_steps(edges, rows):
    requests = len(edges) - 1
    first, steps = [], []
    for b in range(requests):
        begin = lax.div(edges[b], SPAN)
        end = lax.div(edges[b + 1] + (SPAN - 1), SPAN)
        first.append(begin)
        steps.append(jnp.where(edges[b + 1] > edges[b], end - begin, 0))
    offset = [jnp.int32(0)]
    for b in range(requests):
        offset.append(offset[-1] + steps[b])
    lasts = [(steps[b] > 0, jnp.where(steps[b] > 0, offset[b + 1] - 1, 0)) for b in range(requests)]
    entries = []
    for j in range(rows // SPAN + requests - 1):
        request = jnp.int32(0)
        for b in range(1, requests):
            request += (j >= offset[b]).astype(jnp.int32)
        base = pick(request, offset[:-1])
        live = j < offset[-1]
        block = jnp.where(live, pick(request, first) + (j - base), 0)
        begin = block * SPAN
        lower = pick(request, edges[:-1])
        upper = jnp.where(live, pick(request, edges[1:]), 0)
        entries.append((request, block, lower - begin, upper - begin, j == base))
    return entries, lasts


def score_steps(entries, factor, keys, queries, s_ref, m_ref, here):
    columns = iota((1, SPAN), 1)
    for j, (request, block, lower, upper, fresh) in enumerate(entries):
        score = jnp.dot(queries[request, here], keys[block], preferred_element_type=F32)
        score = jnp.where((columns >= lower) & (columns < upper), score * factor, FAR)
        s_ref[j, here] = score
        top = folded(jnp.maximum, score)
        m_ref[j, here] = jnp.where(fresh, top, jnp.maximum(top, m_ref[j - 1, here])) if j else top


def score_extra(lasts, factor, extra, queries, e_ref, m_ref, top_ref, here):
    requests, _, width = queries.shape
    tag = extra[width : width + 1, :].astype(F32)
    for b in range(requests):
        score = jnp.dot(queries[b, here], extra[:width, :], preferred_element_type=F32)
        score = jnp.where(tag == b + 1.0, score * factor, FAR)
        e_ref[b, here] = score
        some, last = lasts[b]
        top = jnp.maximum(folded(jnp.maximum, score), jnp.where(some, m_ref[last, here], FAR))
        top_ref[b, here] = jnp.max(top, axis=1, keepdims=True)


def value_steps(entries, lasts, latent, keys, extra, s_ref, e_ref, top_ref, l_ref, h_ref):
    requests = len(lasts)
    for j, (request, block, _, _, fresh) in enumerate(entries):
        expo = jnp.exp2(s_ref[j] - top_ref[request])
        total = folded(jnp.add, expo)
        part = lax.dot_general(
            expo.astype(BF16), keys[block, :latent], NT, preferred_element_type=F32
        )
        if j:
            keep = jnp.where(fresh, 0.0, 1.0)
            total += l_ref[j - 1] * keep
            part += h_ref[j - 1] * keep
        l_ref[j] = total
        h_ref[j] = part
    sums = []
    for b, (some, last) in enumerate(lasts):
        expo = jnp.exp2(e_ref[b] - top_ref[b])
        keep = jnp.where(some, 1.0, 0.0)
        total = jnp.sum(folded(jnp.add, expo) + l_ref[last] * keep, axis=1, keepdims=True)
        part = lax.dot_general(
            expo.astype(BF16), extra[:latent, :], NT, preferred_element_type=F32
        )
        sums.append((total, part + h_ref[last] * keep))
    return sums


def write_parts(sums, side, top_ref, a_ref, b_ref, st_ref):
    places = early_places(side) + late_places(side)
    units = len(places)
    count, latent = sums[0][1].shape
    lane = iota((count, 128), 1)
    row = lax.rem(iota((count, 128), 0), ROWS)
    tops = jnp.zeros((units, 128), F32)
    tots = jnp.zeros((units, 128), F32)
    for b, (total, whole) in enumerate(sums):
        for u, (dz, dy) in enumerate(places):
            piece = whole[u * ROWS : (u + 1) * ROWS].astype(BF16)
            a_ref[dy, dz, b * ROWS : (b + 1) * ROWS, :] = piece[:, : latent // 2]
            b_ref[dz, dy, b * ROWS : (b + 1) * ROWS, :] = piece[:, latent // 2 :]
        mine = lane == row + b * ROWS
        tops += jnp.sum(
            jnp.where(mine, top_ref[b], 0.0).reshape(units, ROWS, 128), axis=1
        )
        tots += jnp.sum(jnp.where(mine, total, 0.0).reshape(units, ROWS, 128), axis=1)
    for u, (dz, dy) in enumerate(places):
        st_ref[dy, dz, 0:1, :] = tops[u : u + 1]
        st_ref[dy, dz, 1:2, :] = tots[u : u + 1]


def early_places(side):
    return [(0, dy) for dy in range(side)] + [(dz, 0) for dz in range(1, side)]


def late_places(side):
    return [(dz, dy) for dz in range(1, side) for dy in range(1, side)]


def line_up(places, begin, buffer, queries):
    for b in range(queries.shape[0]):
        for u, (dz, dy) in enumerate(places):
            here = slice(begin + u * ROWS, begin + (u + 1) * ROWS)
            queries[b, here, :] = buffer[dz, dy, b * ROWS : (b + 1) * ROWS, :]


def blend(tops):
    top = functools.reduce(jnp.maximum, tops)
    return top, [jnp.exp2(item - top) for item in tops]


def columns_of(weight, rows):
    n = weight.shape[0]
    chosen = iota((n, rows, 128), 2) == iota((n, rows, 128), 1)
    return jnp.sum(jnp.where(chosen, weight[:, None, :], 0.0), axis=2, keepdims=True)


def total_of(tots, weights):
    return functools.reduce(jnp.add, [t * w for t, w in zip(tots, weights)])


def acc_of(accs, columns):
    return functools.reduce(jnp.add, [a.astype(F32) * col for a, col in zip(accs, columns)])


def fused_kernel(
    side,
    n_role,
    scale,
    cache_ref,
    ids_ref,
    rows_ref,
    owner_ref,
    request_ref,
    new_ref,
    nope_ref,
    rope_ref,
    key_ref,
    value_ref,
    out_ref,
    keys,
    key_s,
    value_s,
    rows_s,
    wide,
    fresh_rows,
    packed,
    got,
    extra,
    held,
    mate_held,
    queries,
    mate_queries,
    s_own,
    s_mate,
    e_own,
    e_mate,
    top_own,
    top_mate,
    m_own,
    m_mate,
    l_ref,
    h_ref,
    mine_a,
    mine_b,
    mine_st,
    give_a,
    give_b,
    give_st,
    pair_a,
    pair_b,
    pair_st,
    in1_a,
    in1_b,
    in1_sa,
    in1_sb,
    mid2_a,
    mid2_b,
    mid2_sa,
    mid2_sb,
    in2_a,
    in2_b,
    in2_sa,
    in2_sb,
    send_sem,
    recv_sem,
    local_sem,
):
    g = lax.axis_index("role")
    seq = lax.axis_index("seq")
    y, z, c = place(side)
    others = range(1, side)
    y_peers = [{"role": g, "seq": seq_of(side, turned(y, d, side), z, c)} for d in others]
    z_peers = [{"role": g, "seq": seq_of(side, y, turned(z, d, side), c)} for d in others]
    x_peers = [{"role": turned(g, d, n_role), "seq": seq} for d in range(1, n_role)]
    mate = {"role": g, "seq": seq_of(side, y, z, 1 - c)}
    peers = y_peers + z_peers + x_peers + [mate]

    barrier = pltpu.get_barrier_semaphore()
    for device in peers:
        pl.semaphore_signal(barrier, inc=1, device_id=device, device_id_type=MESH)

    width, rows = cache_ref.shape
    local = []

    def fetch(src, dst):
        copy = pltpu.make_async_copy(src, dst, local_sem.at[len(local)])
        copy.start()
        local.append(copy)
        return copy

    key_copy = fetch(key_ref, key_s)
    rows_copy = fetch(rows_ref, rows_s)
    cache_copies = [
        fetch(cache_ref.at[:, pl.ds(i * SPAN, SPAN)], keys.at[i]) for i in range(rows // SPAN)
    ]
    value_copy = fetch(value_ref, value_s)

    count = [0]
    started = []

    def send(src, dst, device):
        k = count[0]
        count[0] += 1
        copy = pltpu.make_async_remote_copy(
            src_ref=src,
            dst_ref=dst,
            send_sem=send_sem.at[k],
            recv_sem=recv_sem.at[k],
            device_id=device,
            device_id_type=MESH,
        )
        copy.start()
        started.append(copy)
        return copy

    send_count = rows_ref.shape[1]
    devices = n_role * 2 * side * side
    owner = owner_ref[...]
    hits = iota((devices, send_count), 0) == owner
    earlier = iota((send_count, send_count), 0) < iota((send_count, send_count), 1)
    before = jnp.dot(hits.astype(BF16), earlier.astype(BF16), preferred_element_type=F32)
    slot = jnp.sum(jnp.where(hits, before, 0.0), axis=0, keepdims=True).astype(jnp.int32)
    position = owner * CAP + slot
    chosen = (iota((devices * CAP, send_count), 0) == position).astype(BF16)
    room = packed.shape[2]
    marked = jnp.broadcast_to((request_ref[...] + 1).astype(BF16), (ROWS, send_count))
    rows_copy.wait()
    for i in range(n_role):
        part = chosen[i * room : (i + 1) * room]
        packed[i, :width] = lax.dot_general(
            rows_s[...], part, NT, preferred_element_type=F32
        ).astype(BF16)
        packed[i, width:] = lax.dot_general(
            marked, part, NT, preferred_element_type=F32
        ).astype(BF16)

    latent = key_ref.shape[2]
    half = latent // 2
    x_nope = gather_rows(nope_ref, wide)
    key_copy.wait()
    held[0, 0, :, :latent] = absorb_queries(x_nope, key_s)
    held[0, 0, :, latent:] = gather_rows(rope_ref, wide)

    pl.semaphore_wait(barrier, len(peers))

    piece = held.at[0, 0]
    first = []
    for d in others:
        first.append(send(piece, held.at[0, side - d], y_peers[d - 1]))
        first.append(send(piece, held.at[side - d, 0], z_peers[d - 1]))
    crossing = [
        send(packed.at[turned(g, d, n_role)], got.at[n_role - d - 1], x_peers[d - 1])
        for d in range(1, n_role)
    ]
    extra[:, :room] = packed[g]

    own_rows = held.shape[2]
    own_query = held[0, 0]
    requests, steps, _ = new_ref.shape
    heads = key_ref.shape[0]
    factor = scale * LOG2E
    for b in range(requests):
        fresh_rows[b * steps : (b + 1) * steps, :] = new_ref[b].astype(F32)
    new = fresh_rows[...].astype(BF16)
    score = lax.dot_general(own_query, new, NT, preferred_element_type=F32) * factor
    r_row, r_col = iota(score.shape, 0), iota(score.shape, 1)
    seen = (lax.div(r_row, ROWS) == lax.div(r_col, steps)) & (
        lax.div(lax.rem(r_row, ROWS), heads) >= lax.rem(r_col, steps)
    )
    top0 = jnp.max(jnp.where(seen, score, FAR), axis=1, keepdims=True)
    expo = jnp.where(seen, jnp.exp2(score - top0), 0.0)
    tot0 = jnp.sum(expo, axis=1, keepdims=True)
    acc0 = jnp.dot(expo.astype(BF16), new[:, :latent], preferred_element_type=F32)

    ids = ids_ref[...]
    edges = [jnp.int32(0)]
    for b in range(1, requests):
        edges.append(jnp.sum((ids < b).astype(jnp.int32)))
    edges.append(jnp.int32(rows))

    entries, lasts = plan_steps(edges, rows)

    for copy in first:
        copy.wait_recv()
    rest = pl.ds(1, side - 1)
    second = []
    for d in others:
        src, dst = held.at[0, rest, :, :half], held.at[side - d, rest, :, :half]
        second.append(send(src, dst, z_peers[d - 1]))
        src, dst = held.at[rest, 0, :, half:], held.at[rest, side - d, :, half:]
        second.append(send(src, dst, y_peers[d - 1]))
    across = [
        send(held.at[0], mate_held.at[0], mate),
        send(held.at[rest, 0], mate_held.at[rest, 0], mate),
    ]

    early, late = early_places(side), late_places(side)
    split = len(early) * ROWS
    total_rows = queries.shape[1]
    soon, later = slice(0, split), slice(split, total_rows)
    for copy in cache_copies:
        copy.wait()
    line_up(early, 0, held, queries)
    score_steps(entries, factor, keys, queries, s_own, m_own, soon)
    for copy in across:
        copy.wait_recv()
    line_up(early, 0, mate_held, mate_queries)
    score_steps(entries, factor, keys, mate_queries, s_mate, m_mate, soon)
    for copy in crossing:
        copy.wait_recv()
    for i in range(1, n_role):
        extra[:, i * room : (i + 1) * room] = got[i - 1]

    for copy in second:
        copy.wait_recv()
    tail = send(held.at[rest, rest], mate_held.at[rest, rest], mate)
    score_extra(lasts, factor, extra, queries, e_own, m_own, top_own, soon)
    score_extra(lasts, factor, extra, mate_queries, e_mate, m_mate, top_mate, soon)
    line_up(late, split, held, queries)
    score_steps(entries, factor, keys, queries, s_own, m_own, later)
    tail.wait_recv()
    line_up(late, split, mate_held, mate_queries)
    score_steps(entries, factor, keys, mate_queries, s_mate, m_mate, later)
    score_extra(lasts, factor, extra, mate_queries, e_mate, m_mate, top_mate, later)
    sums = value_steps(
        entries, lasts, latent, keys, extra, s_mate, e_mate, top_mate, l_ref, h_ref
    )
    write_parts(sums, side, top_mate, give_a, give_b, give_st)
    halves = [
        send(give_a, pair_a, mate),
        send(give_b, pair_b, mate),
        send(give_st, pair_st, mate),
    ]
    score_extra(lasts, factor, extra, queries, e_own, m_own, top_own, later)
    sums = value_steps(
        entries, lasts, latent, keys, extra, s_own, e_own, top_own, l_ref, h_ref
    )
    write_parts(sums, side, top_own, mine_a, mine_b, mine_st)
    for copy in halves:
        copy.wait_recv()

    for i in range(side):
        top, weights = blend([mine_st[i, :, 0, :], pair_st[i, :, 0, :]])
        columns = [columns_of(w, own_rows) for w in weights]
        total = total_of([mine_st[i, :, 1, :], pair_st[i, :, 1, :]], weights)
        mine_st[i, :, 0, :] = top
        mine_st[i, :, 1, :] = total
        mine_a[i] = acc_of([mine_a[i], pair_a[i]], columns).astype(BF16)
        for k in range(side):
            mine_b[k, i] = acc_of(
                [mine_b[k, i], pair_b[k, i]], [col[k] for col in columns]
            ).astype(BF16)

    over_a, over_b = [], []
    before_over = len(started)
    for d in others:
        over_a.append(send(mine_a.at[d], in1_a.at[d - 1], y_peers[d - 1]))
        over_b.append(send(mine_b.at[d], in1_b.at[d - 1], z_peers[d - 1]))
        over_a.append(send(mine_st.at[d], in1_sa.at[d - 1], y_peers[d - 1]))
        over_b.append(send(mine_st.at[:, d], in1_sb.at[d - 1], z_peers[d - 1]))

    def flush(until):
        for copy in started[flushed[0] : until]:
            copy.wait_send()
        flushed[0] = until

    flushed = [0]
    flush(before_over)

    def settle(copies, mine_acc, mine_stat, in_acc, in_stat):
        for copy in copies:
            copy.wait_recv()
        stats = [mine_stat] + [in_stat[d] for d in range(side - 1)]
        top, weights = blend([s[:, 0, :] for s in stats])
        columns = [columns_of(w, own_rows) for w in weights]
        total = total_of([s[:, 1, :] for s in stats], weights)
        acc = acc_of([mine_acc] + [in_acc[d] for d in range(side - 1)], columns)
        return top, total, acc

    top, total, acc = settle(over_a, mine_a[0], mine_st[0], in1_a, in1_sa)
    mid2_sa[:, 0, :] = top
    mid2_sa[:, 1, :] = total
    mid2_a[...] = acc.astype(BF16)
    next_a, next_b = [], []
    before_next = len(started)
    for d in others:
        next_a.append(send(mid2_a.at[d], in2_a.at[d - 1], z_peers[d - 1]))
        next_a.append(send(mid2_sa.at[d], in2_sa.at[d - 1], z_peers[d - 1]))
    top, total, acc = settle(over_b, mine_b[0], mine_st[:, 0], in1_b, in1_sb)
    mid2_sb[:, 0, :] = top
    mid2_sb[:, 1, :] = total
    mid2_b[...] = acc.astype(BF16)
    for d in others:
        next_b.append(send(mid2_b.at[d], in2_b.at[d - 1], y_peers[d - 1]))
        next_b.append(send(mid2_sb.at[d], in2_sb.at[d - 1], y_peers[d - 1]))

    flush(before_next)

    def finish(copies, mine_acc, mine_stat, in_acc, in_stat, fresh_acc):
        for copy in copies:
            copy.wait_recv()
        stats = [mine_stat] + [in_stat[d] for d in range(side - 1)]
        top, weights = blend([s[0:1, :] for s in stats])
        columns = [columns_of(w, own_rows)[0] for w in weights]
        total = total_of([s[1:2, :] for s in stats], weights)
        acc = acc_of([mine_acc] + [in_acc[d] for d in range(side - 1)], columns)
        top_c, tot_c = columns_of(top, own_rows)[0], columns_of(total, own_rows)[0]
        best = jnp.maximum(top_c, top0)
        keep_c, keep_0 = jnp.exp2(top_c - best), jnp.exp2(top0 - best)
        tot = tot_c * keep_c + tot0 * keep_0
        return ((acc * keep_c + fresh_acc * keep_0) / tot).astype(BF16)

    value_copy.wait()
    out_a = finish(next_a, mid2_a[0], mid2_sa[0], in2_a, in2_sa, acc0[:, : latent // 2])
    out_b = finish(next_b, mid2_b[0], mid2_sb[0], in2_b, in2_sb, acc0[:, latent // 2 :])
    head = lax.rem(iota((own_rows, 1), 0), heads)
    result = jnp.zeros((own_rows, value_ref.shape[2]), F32)
    for h in range(heads):
        part = jnp.dot(out_a, value_s[h, : latent // 2], preferred_element_type=F32)
        part += jnp.dot(out_b, value_s[h, latent // 2 :], preferred_element_type=F32)
        result = result + jnp.where(head == h, part, 0.0)
    for t in range(steps):
        for b in range(requests):
            begin = (b * steps + t) * heads
            out_ref[t, b] = result[begin : begin + heads].astype(BF16)

    flush(len(started))


def per_device(
    cache_rows,
    cache_request,
    sent_rows,
    sent_owner,
    sent_request,
    new_rows,
    query_nope,
    query_rope,
    absorb_key,
    absorb_value,
):
    n_role = lax.axis_size("role")
    n_seq = lax.axis_size("seq")
    side = 1
    while 2 * side * side < n_seq:
        side += 1
    steps, requests, heads, nope = query_nope.shape
    rope = query_rope.shape[3]
    latent = absorb_key.shape[2]
    width = sent_rows.shape[1]
    half = latent // 2
    own = steps * requests * heads
    send = sent_rows.shape[0]
    room = CAP * n_seq
    scale = 1.0 / float(nope + rope) ** 0.5
    local_rows = cache_rows.shape[1]
    units = side * side
    count = units * steps * heads
    listed = local_rows // SPAN + requests - 1

    vmem = pl.BlockSpec(memory_space=pltpu.VMEM)
    hbm = pl.BlockSpec(memory_space=pl.ANY)
    dma = pltpu.SemaphoreType.DMA
    grid = (side, side)
    far = side - 1

    def bf16(*shape):
        return pltpu.VMEM(shape, BF16)

    def f32(*shape):
        return pltpu.VMEM(shape, F32)

    copies = 12 * far + (n_role - 1) + 3 + 3
    return pl.pallas_call(
        functools.partial(fused_kernel, side, n_role, scale),
        out_shape=jax.ShapeDtypeStruct((steps, requests, heads, absorb_value.shape[2]), BF16),
        in_specs=[hbm, vmem, hbm, vmem, vmem, vmem, vmem, vmem, hbm, hbm],
        out_specs=vmem,
        scratch_shapes=[
            bf16(local_rows // SPAN, width, SPAN),
            bf16(heads, nope, latent),
            bf16(heads, latent, absorb_value.shape[2]),
            bf16(width, send),
            f32(own, nope),
            f32(steps * requests, width),
            bf16(n_role, width + ROWS, room),
            bf16(n_role - 1, width + ROWS, room),
            bf16(width + ROWS, n_role * room),
            bf16(side, side, own, width),
            bf16(side, side, own, width),
            bf16(requests, count, width),
            bf16(requests, count, width),
            f32(listed, count, SPAN),
            f32(listed, count, SPAN),
            f32(requests, count, n_role * room),
            f32(requests, count, n_role * room),
            f32(requests, count, 1),
            f32(requests, count, 1),
            f32(listed, count, 128),
            f32(listed, count, 128),
            f32(listed, count, 128),
            f32(listed, count, latent),
            bf16(side, side, own, half),
            bf16(side, side, own, half),
            f32(side, side, 2, 128),
            bf16(side, side, own, half),
            bf16(side, side, own, half),
            f32(side, side, 2, 128),
            bf16(side, side, own, half),
            bf16(side, side, own, half),
            f32(side, side, 2, 128),
            bf16(far, side, own, half),
            bf16(far, side, own, half),
            f32(far, side, 2, 128),
            f32(far, side, 2, 128),
            bf16(side, own, half),
            bf16(side, own, half),
            f32(side, 2, 128),
            f32(side, 2, 128),
            bf16(far, own, half),
            bf16(far, own, half),
            f32(far, 2, 128),
            f32(far, 2, 128),
            dma((copies,)),
            dma((copies,)),
            dma((local_rows // SPAN + 3,)),
        ],
        compiler_params=pltpu.CompilerParams(
            collective_id=0, has_side_effects=True, vmem_limit_bytes=VMEM_BYTES
        ),
        name="fused",
    )(
        cache_rows[0].T,
        cache_request,
        sent_rows.T,
        sent_owner.reshape(1, send),
        sent_request.reshape(1, send),
        jnp.transpose(new_rows, (1, 0, 2)),
        query_nope,
        query_rope,
        absorb_key,
        absorb_value,
    )


def solution(mesh):
    placed = (
        P("role", "seq", None),
        P("role", "seq"),
        P(("role", "seq"), None),
        P(("role", "seq"), None),
        P(("role", "seq")),
        P(None, "role", None),
        P(None, "role", "seq", None),
        P(None, "role", "seq", None),
        P("seq", None, None),
        P("seq", None, None),
    )
    return jax.shard_map(
        per_device,
        mesh=mesh,
        in_specs=placed,
        out_specs=P(None, "role", "seq", None),
        check_vma=False,
    )
```

```python
import functools

import jax
import jax.numpy as jnp
from jax import lax
from jax.experimental import pallas as pl
from jax.experimental.pallas import tpu as pltpu
from jax.sharding import PartitionSpec as P

FAR = -1e30
LOG2E = 1.4426950408889634
MESH = pl.DeviceIdType.MESH
F32 = jnp.float32
BF16 = jnp.bfloat16
NT = (((1,), (1,)), ((), ()))

CAP = 4
SPAN = 512
ROWS = 16
VMEM_BYTES = 56 * 1024 * 1024


def iota(shape, dim):
    return lax.broadcasted_iota(jnp.int32, shape, dim)


def place(side):
    seq = lax.axis_index("seq")
    return lax.div(seq, 2 * side), lax.rem(lax.div(seq, 2), side), lax.rem(seq, 2)


def seq_of(side, y, z, c):
    return (y * side + z) * 2 + c


def turned(value, by, size):
    return lax.rem(value + by, size)


def absorb_queries(nope, key_ref):
    rows = nope.shape[0]
    heads = key_ref.shape[0]
    head = lax.rem(iota((rows, 1), 0), heads)
    total = jnp.zeros((rows, key_ref.shape[2]), F32)
    for h in range(heads):
        part = jnp.dot(nope, key_ref[h], preferred_element_type=F32)
        total = total + jnp.where(head == h, part, 0.0)
    return total.astype(BF16)


def gather_rows(source_ref, wide):
    steps, requests, heads, n = source_ref.shape
    for t in range(steps):
        for r in range(requests):
            begin = (r * steps + t) * heads
            wide[begin : begin + heads, :n] = source_ref[t, r].astype(F32)
    return wide[:, :n].astype(BF16)


def pick(index, values):
    result = values[-1]
    for b in reversed(range(len(values) - 1)):
        result = jnp.where(index == b, values[b], result)
    return result


def folded(combine, wide):
    return functools.reduce(combine, [wide[:, i : i + 128] for i in range(0, wide.shape[1], 128)])


def plan_steps(edges, rows):
    requests = len(edges) - 1
    first, steps = [], []
    for b in range(requests):
        begin = lax.div(edges[b], SPAN)
        end = lax.div(edges[b + 1] + (SPAN - 1), SPAN)
        first.append(begin)
        steps.append(jnp.where(edges[b + 1] > edges[b], end - begin, 0))
    offset = [jnp.int32(0)]
    for b in range(requests):
        offset.append(offset[-1] + steps[b])
    lasts = [(steps[b] > 0, jnp.where(steps[b] > 0, offset[b + 1] - 1, 0)) for b in range(requests)]
    entries = []
    for j in range(rows // SPAN + requests - 1):
        request = jnp.int32(0)
        for b in range(1, requests):
            request += (j >= offset[b]).astype(jnp.int32)
        base = pick(request, offset[:-1])
        live = j < offset[-1]
        block = jnp.where(live, pick(request, first) + (j - base), 0)
        begin = block * SPAN
        lower = pick(request, edges[:-1])
        upper = jnp.where(live, pick(request, edges[1:]), 0)
        entries.append((request, block, lower - begin, upper - begin, j == base))
    return entries, lasts


def score_steps(entries, factor, keys, queries, s_ref, m_ref, here):
    columns = iota((1, SPAN), 1)
    for j, (request, block, lower, upper, fresh) in enumerate(entries):
        score = jnp.dot(queries[request, here], keys[block], preferred_element_type=F32)
        score = jnp.where((columns >= lower) & (columns < upper), score * factor, FAR)
        s_ref[j, here] = score
        top = folded(jnp.maximum, score)
        m_ref[j, here] = jnp.where(fresh, top, jnp.maximum(top, m_ref[j - 1, here])) if j else top


def score_extra(lasts, factor, extra, queries, e_ref, m_ref, top_ref, here):
    requests, _, width = queries.shape
    tag = extra[width : width + 1, :].astype(F32)
    for b in range(requests):
        score = jnp.dot(queries[b, here], extra[:width, :], preferred_element_type=F32)
        score = jnp.where(tag == b + 1.0, score * factor, FAR)
        e_ref[b, here] = score
        some, last = lasts[b]
        top = jnp.maximum(folded(jnp.maximum, score), jnp.where(some, m_ref[last, here], FAR))
        top_ref[b, here] = jnp.max(top, axis=1, keepdims=True)


def value_steps(entries, lasts, latent, keys, extra, s_ref, e_ref, top_ref, l_ref, h_ref):
    requests = len(lasts)
    for j, (request, block, _, _, fresh) in enumerate(entries):
        expo = jnp.exp2(s_ref[j] - top_ref[request])
        total = folded(jnp.add, expo)
        part = lax.dot_general(
            expo.astype(BF16), keys[block, :latent], NT, preferred_element_type=F32
        )
        if j:
            keep = jnp.where(fresh, 0.0, 1.0)
            total += l_ref[j - 1] * keep
            part += h_ref[j - 1] * keep
        l_ref[j] = total
        h_ref[j] = part
    sums = []
    for b, (some, last) in enumerate(lasts):
        expo = jnp.exp2(e_ref[b] - top_ref[b])
        keep = jnp.where(some, 1.0, 0.0)
        total = jnp.sum(folded(jnp.add, expo) + l_ref[last] * keep, axis=1, keepdims=True)
        part = lax.dot_general(
            expo.astype(BF16), extra[:latent, :], NT, preferred_element_type=F32
        )
        sums.append((total, part + h_ref[last] * keep))
    return sums


def write_parts(sums, side, top_ref, a_ref, b_ref, st_ref):
    places = early_places(side) + late_places(side)
    units = len(places)
    count, latent = sums[0][1].shape
    lane = iota((count, 128), 1)
    row = lax.rem(iota((count, 128), 0), ROWS)
    tops = jnp.zeros((units, 128), F32)
    tots = jnp.zeros((units, 128), F32)
    for b, (total, whole) in enumerate(sums):
        for u, (dz, dy) in enumerate(places):
            piece = whole[u * ROWS : (u + 1) * ROWS].astype(BF16)
            a_ref[dy, dz, b * ROWS : (b + 1) * ROWS, :] = piece[:, : latent // 2]
            b_ref[dz, dy, b * ROWS : (b + 1) * ROWS, :] = piece[:, latent // 2 :]
        mine = lane == row + b * ROWS
        tops += jnp.sum(
            jnp.where(mine, top_ref[b], 0.0).reshape(units, ROWS, 128), axis=1
        )
        tots += jnp.sum(jnp.where(mine, total, 0.0).reshape(units, ROWS, 128), axis=1)
    for u, (dz, dy) in enumerate(places):
        st_ref[dy, dz, 0:1, :] = tops[u : u + 1]
        st_ref[dy, dz, 1:2, :] = tots[u : u + 1]


def early_places(side):
    return [(0, dy) for dy in range(side)] + [(dz, 0) for dz in range(1, side)]


def late_places(side):
    return [(dz, dy) for dz in range(1, side) for dy in range(1, side)]


def line_up(places, begin, buffer, queries):
    for b in range(queries.shape[0]):
        for u, (dz, dy) in enumerate(places):
            here = slice(begin + u * ROWS, begin + (u + 1) * ROWS)
            queries[b, here, :] = buffer[dz, dy, b * ROWS : (b + 1) * ROWS, :]


def blend(tops):
    top = functools.reduce(jnp.maximum, tops)
    return top, [jnp.exp2(item - top) for item in tops]


def columns_of(weight, rows):
    n = weight.shape[0]
    chosen = iota((n, rows, 128), 2) == iota((n, rows, 128), 1)
    return jnp.sum(jnp.where(chosen, weight[:, None, :], 0.0), axis=2, keepdims=True)


def total_of(tots, weights):
    return functools.reduce(jnp.add, [t * w for t, w in zip(tots, weights)])


def acc_of(accs, columns):
    return functools.reduce(jnp.add, [a.astype(F32) * col for a, col in zip(accs, columns)])


def fused_kernel(
    side,
    n_role,
    scale,
    cache_ref,
    ids_ref,
    rows_ref,
    owner_ref,
    request_ref,
    new_ref,
    nope_ref,
    rope_ref,
    key_ref,
    value_ref,
    out_ref,
    keys,
    key_s,
    value_s,
    rows_s,
    wide,
    fresh_rows,
    packed,
    got,
    extra,
    held,
    mate_held,
    queries,
    mate_queries,
    s_own,
    s_mate,
    e_own,
    e_mate,
    top_own,
    top_mate,
    m_own,
    m_mate,
    l_ref,
    h_ref,
    mine_a,
    mine_b,
    mine_st,
    give_a,
    give_b,
    give_st,
    pair_a,
    pair_b,
    pair_st,
    in1_a,
    in1_b,
    in1_sa,
    in1_sb,
    mid2_a,
    mid2_b,
    mid2_sa,
    mid2_sb,
    in2_a,
    in2_b,
    in2_sa,
    in2_sb,
    send_sem,
    recv_sem,
    local_sem,
):
    g = lax.axis_index("role")
    seq = lax.axis_index("seq")
    y, z, c = place(side)
    others = range(1, side)
    far_first = sorted(others, key=lambda d: -min(d, side - d))
    y_peers = [{"role": g, "seq": seq_of(side, turned(y, d, side), z, c)} for d in others]
    z_peers = [{"role": g, "seq": seq_of(side, y, turned(z, d, side), c)} for d in others]
    x_peers = [{"role": turned(g, d, n_role), "seq": seq} for d in range(1, n_role)]
    mate = {"role": g, "seq": seq_of(side, y, z, 1 - c)}
    peers = y_peers + z_peers + x_peers + [mate]

    barrier = pltpu.get_barrier_semaphore()
    for device in peers:
        pl.semaphore_signal(barrier, inc=1, device_id=device, device_id_type=MESH)

    width, rows = cache_ref.shape
    local = []

    def fetch(src, dst):
        copy = pltpu.make_async_copy(src, dst, local_sem.at[len(local)])
        copy.start()
        local.append(copy)
        return copy

    key_copy = fetch(key_ref, key_s)
    rows_copy = fetch(rows_ref, rows_s)
    cache_copies = [
        fetch(cache_ref.at[:, pl.ds(i * SPAN, SPAN)], keys.at[i]) for i in range(rows // SPAN)
    ]
    value_copy = fetch(value_ref, value_s)

    count = [0]
    started = []

    def send(src, dst, device):
        k = count[0]
        count[0] += 1
        copy = pltpu.make_async_remote_copy(
            src_ref=src,
            dst_ref=dst,
            send_sem=send_sem.at[k],
            recv_sem=recv_sem.at[k],
            device_id=device,
            device_id_type=MESH,
        )
        copy.start()
        started.append(copy)
        return copy

    send_count = rows_ref.shape[1]
    devices = n_role * 2 * side * side
    owner = owner_ref[...]
    hits = iota((devices, send_count), 0) == owner
    earlier = iota((send_count, send_count), 0) < iota((send_count, send_count), 1)
    before = jnp.dot(hits.astype(BF16), earlier.astype(BF16), preferred_element_type=F32)
    slot = jnp.sum(jnp.where(hits, before, 0.0), axis=0, keepdims=True).astype(jnp.int32)
    position = owner * CAP + slot
    chosen = (iota((devices * CAP, send_count), 0) == position).astype(BF16)
    room = packed.shape[2]
    marked = jnp.broadcast_to((request_ref[...] + 1).astype(BF16), (ROWS, send_count))
    rows_copy.wait()
    for i in range(n_role):
        part = chosen[i * room : (i + 1) * room]
        packed[i, :width] = lax.dot_general(
            rows_s[...], part, NT, preferred_element_type=F32
        ).astype(BF16)
        packed[i, width:] = lax.dot_general(
            marked, part, NT, preferred_element_type=F32
        ).astype(BF16)

    latent = key_ref.shape[2]
    half = latent // 2
    x_nope = gather_rows(nope_ref, wide)
    key_copy.wait()
    held[0, 0, :, :latent] = absorb_queries(x_nope, key_s)
    held[0, 0, :, latent:] = gather_rows(rope_ref, wide)

    pl.semaphore_wait(barrier, len(peers))

    piece = held.at[0, 0]
    first = []
    for d in far_first:
        first.append(send(piece, held.at[0, side - d], y_peers[d - 1]))
        first.append(send(piece, held.at[side - d, 0], z_peers[d - 1]))
    crossing = [
        send(packed.at[turned(g, d, n_role)], got.at[n_role - d - 1], x_peers[d - 1])
        for d in range(1, n_role)
    ]
    extra[:, :room] = packed[g]

    own_rows = held.shape[2]
    own_query = held[0, 0]
    requests, steps, _ = new_ref.shape
    heads = key_ref.shape[0]
    factor = scale * LOG2E
    for b in range(requests):
        fresh_rows[b * steps : (b + 1) * steps, :] = new_ref[b].astype(F32)
    new = fresh_rows[...].astype(BF16)
    score = lax.dot_general(own_query, new, NT, preferred_element_type=F32) * factor
    r_row, r_col = iota(score.shape, 0), iota(score.shape, 1)
    seen = (lax.div(r_row, ROWS) == lax.div(r_col, steps)) & (
        lax.div(lax.rem(r_row, ROWS), heads) >= lax.rem(r_col, steps)
    )
    top0 = jnp.max(jnp.where(seen, score, FAR), axis=1, keepdims=True)
    expo = jnp.where(seen, jnp.exp2(score - top0), 0.0)
    tot0 = jnp.sum(expo, axis=1, keepdims=True)
    acc0 = jnp.dot(expo.astype(BF16), new[:, :latent], preferred_element_type=F32)

    ids = ids_ref[...]
    edges = [jnp.int32(0)]
    for b in range(1, requests):
        edges.append(jnp.sum((ids < b).astype(jnp.int32)))
    edges.append(jnp.int32(rows))

    entries, lasts = plan_steps(edges, rows)

    for copy in first:
        copy.wait_recv()
    rest = pl.ds(1, side - 1)
    second = []
    for d in far_first:
        src, dst = held.at[0, rest, :, :half], held.at[side - d, rest, :, :half]
        second.append(send(src, dst, z_peers[d - 1]))
        src, dst = held.at[rest, 0, :, half:], held.at[rest, side - d, :, half:]
        second.append(send(src, dst, y_peers[d - 1]))
    across = [
        send(held.at[0], mate_held.at[0], mate),
        send(held.at[rest, 0], mate_held.at[rest, 0], mate),
    ]

    early, late = early_places(side), late_places(side)
    split = len(early) * ROWS
    total_rows = queries.shape[1]
    soon, later = slice(0, split), slice(split, total_rows)
    for copy in cache_copies:
        copy.wait()
    line_up(early, 0, held, queries)
    score_steps(entries, factor, keys, queries, s_own, m_own, soon)
    for copy in across:
        copy.wait_recv()
    line_up(early, 0, mate_held, mate_queries)
    score_steps(entries, factor, keys, mate_queries, s_mate, m_mate, soon)
    for copy in crossing:
        copy.wait_recv()
    for i in range(1, n_role):
        extra[:, i * room : (i + 1) * room] = got[i - 1]

    score_extra(lasts, factor, extra, queries, e_own, m_own, top_own, soon)
    score_extra(lasts, factor, extra, mate_queries, e_mate, m_mate, top_mate, soon)
    for copy in second:
        copy.wait_recv()
    tail = send(held.at[rest, rest], mate_held.at[rest, rest], mate)
    line_up(late, split, held, queries)
    score_steps(entries, factor, keys, queries, s_own, m_own, later)
    tail.wait_recv()
    line_up(late, split, mate_held, mate_queries)
    score_steps(entries, factor, keys, mate_queries, s_mate, m_mate, later)
    score_extra(lasts, factor, extra, mate_queries, e_mate, m_mate, top_mate, later)
    sums = value_steps(
        entries, lasts, latent, keys, extra, s_mate, e_mate, top_mate, l_ref, h_ref
    )
    write_parts(sums, side, top_mate, give_a, give_b, give_st)
    halves = [
        send(give_a, pair_a, mate),
        send(give_b, pair_b, mate),
        send(give_st, pair_st, mate),
    ]
    score_extra(lasts, factor, extra, queries, e_own, m_own, top_own, later)
    sums = value_steps(
        entries, lasts, latent, keys, extra, s_own, e_own, top_own, l_ref, h_ref
    )
    write_parts(sums, side, top_own, mine_a, mine_b, mine_st)
    for copy in halves:
        copy.wait_recv()

    over_a, over_b = [], []
    before_over = len(started)
    for i in far_first + [0]:
        top, weights = blend([mine_st[i, :, 0, :], pair_st[i, :, 0, :]])
        columns = [columns_of(w, own_rows) for w in weights]
        total = total_of([mine_st[i, :, 1, :], pair_st[i, :, 1, :]], weights)
        mine_st[i, :, 0, :] = top
        mine_st[i, :, 1, :] = total
        mine_a[i] = acc_of([mine_a[i], pair_a[i]], columns).astype(BF16)
        for k in range(side):
            mine_b[k, i] = acc_of(
                [mine_b[k, i], pair_b[k, i]], [col[k] for col in columns]
            ).astype(BF16)
        if i:
            over_a.append(send(mine_a.at[i], in1_a.at[i - 1], y_peers[i - 1]))
            over_a.append(send(mine_st.at[i], in1_sa.at[i - 1], y_peers[i - 1]))
    for d in far_first:
        over_b.append(send(mine_b.at[d], in1_b.at[d - 1], z_peers[d - 1]))
        over_b.append(send(mine_st.at[:, d], in1_sb.at[d - 1], z_peers[d - 1]))

    def flush(until):
        for copy in started[flushed[0] : until]:
            copy.wait_send()
        flushed[0] = until

    flushed = [0]
    flush(before_over)

    def settle(copies, mine_acc, mine_stat, in_acc, in_stat):
        for copy in copies:
            copy.wait_recv()
        stats = [mine_stat] + [in_stat[d] for d in range(side - 1)]
        top, weights = blend([s[:, 0, :] for s in stats])
        columns = [columns_of(w, own_rows) for w in weights]
        total = total_of([s[:, 1, :] for s in stats], weights)
        acc = acc_of([mine_acc] + [in_acc[d] for d in range(side - 1)], columns)
        return top, total, acc

    top, total, acc = settle(over_a, mine_a[0], mine_st[0], in1_a, in1_sa)
    mid2_sa[:, 0, :] = top
    mid2_sa[:, 1, :] = total
    mid2_a[...] = acc.astype(BF16)
    next_a, next_b = [], []
    before_next = len(started)
    for d in far_first:
        next_a.append(send(mid2_a.at[d], in2_a.at[d - 1], z_peers[d - 1]))
        next_a.append(send(mid2_sa.at[d], in2_sa.at[d - 1], z_peers[d - 1]))
    top, total, acc = settle(over_b, mine_b[0], mine_st[:, 0], in1_b, in1_sb)
    mid2_sb[:, 0, :] = top
    mid2_sb[:, 1, :] = total
    mid2_b[...] = acc.astype(BF16)
    for d in far_first:
        next_b.append(send(mid2_b.at[d], in2_b.at[d - 1], y_peers[d - 1]))
        next_b.append(send(mid2_sb.at[d], in2_sb.at[d - 1], y_peers[d - 1]))

    flush(before_next)

    def finish(copies, mine_acc, mine_stat, in_acc, in_stat, fresh_acc):
        for copy in copies:
            copy.wait_recv()
        stats = [mine_stat] + [in_stat[d] for d in range(side - 1)]
        top, weights = blend([s[0:1, :] for s in stats])
        columns = [columns_of(w, own_rows)[0] for w in weights]
        total = total_of([s[1:2, :] for s in stats], weights)
        acc = acc_of([mine_acc] + [in_acc[d] for d in range(side - 1)], columns)
        top_c, tot_c = columns_of(top, own_rows)[0], columns_of(total, own_rows)[0]
        best = jnp.maximum(top_c, top0)
        keep_c, keep_0 = jnp.exp2(top_c - best), jnp.exp2(top0 - best)
        tot = tot_c * keep_c + tot0 * keep_0
        return ((acc * keep_c + fresh_acc * keep_0) / tot).astype(BF16)

    value_copy.wait()
    out_a = finish(next_a, mid2_a[0], mid2_sa[0], in2_a, in2_sa, acc0[:, : latent // 2])
    out_b = finish(next_b, mid2_b[0], mid2_sb[0], in2_b, in2_sb, acc0[:, latent // 2 :])
    head = lax.rem(iota((own_rows, 1), 0), heads)
    result = jnp.zeros((own_rows, value_ref.shape[2]), F32)
    for h in range(heads):
        part = jnp.dot(out_a, value_s[h, : latent // 2], preferred_element_type=F32)
        part += jnp.dot(out_b, value_s[h, latent // 2 :], preferred_element_type=F32)
        result = result + jnp.where(head == h, part, 0.0)
    for t in range(steps):
        for b in range(requests):
            begin = (b * steps + t) * heads
            out_ref[t, b] = result[begin : begin + heads].astype(BF16)

    flush(len(started))


def per_device(
    cache_rows,
    cache_request,
    sent_rows,
    sent_owner,
    sent_request,
    new_rows,
    query_nope,
    query_rope,
    absorb_key,
    absorb_value,
):
    n_role = lax.axis_size("role")
    n_seq = lax.axis_size("seq")
    side = 1
    while 2 * side * side < n_seq:
        side += 1
    steps, requests, heads, nope = query_nope.shape
    rope = query_rope.shape[3]
    latent = absorb_key.shape[2]
    width = sent_rows.shape[1]
    half = latent // 2
    own = steps * requests * heads
    send = sent_rows.shape[0]
    room = CAP * n_seq
    scale = 1.0 / float(nope + rope) ** 0.5
    local_rows = cache_rows.shape[1]
    units = side * side
    count = units * steps * heads
    listed = local_rows // SPAN + requests - 1

    vmem = pl.BlockSpec(memory_space=pltpu.VMEM)
    hbm = pl.BlockSpec(memory_space=pl.ANY)
    dma = pltpu.SemaphoreType.DMA
    grid = (side, side)
    far = side - 1

    def bf16(*shape):
        return pltpu.VMEM(shape, BF16)

    def f32(*shape):
        return pltpu.VMEM(shape, F32)

    copies = 12 * far + (n_role - 1) + 3 + 3
    return pl.pallas_call(
        functools.partial(fused_kernel, side, n_role, scale),
        out_shape=jax.ShapeDtypeStruct((steps, requests, heads, absorb_value.shape[2]), BF16),
        in_specs=[hbm, vmem, hbm, vmem, vmem, vmem, vmem, vmem, hbm, hbm],
        out_specs=vmem,
        scratch_shapes=[
            bf16(local_rows // SPAN, width, SPAN),
            bf16(heads, nope, latent),
            bf16(heads, latent, absorb_value.shape[2]),
            bf16(width, send),
            f32(own, nope),
            f32(steps * requests, width),
            bf16(n_role, width + ROWS, room),
            bf16(n_role - 1, width + ROWS, room),
            bf16(width + ROWS, n_role * room),
            bf16(side, side, own, width),
            bf16(side, side, own, width),
            bf16(requests, count, width),
            bf16(requests, count, width),
            f32(listed, count, SPAN),
            f32(listed, count, SPAN),
            f32(requests, count, n_role * room),
            f32(requests, count, n_role * room),
            f32(requests, count, 1),
            f32(requests, count, 1),
            f32(listed, count, 128),
            f32(listed, count, 128),
            f32(listed, count, 128),
            f32(listed, count, latent),
            bf16(side, side, own, half),
            bf16(side, side, own, half),
            f32(side, side, 2, 128),
            bf16(side, side, own, half),
            bf16(side, side, own, half),
            f32(side, side, 2, 128),
            bf16(side, side, own, half),
            bf16(side, side, own, half),
            f32(side, side, 2, 128),
            bf16(far, side, own, half),
            bf16(far, side, own, half),
            f32(far, side, 2, 128),
            f32(far, side, 2, 128),
            bf16(side, own, half),
            bf16(side, own, half),
            f32(side, 2, 128),
            f32(side, 2, 128),
            bf16(far, own, half),
            bf16(far, own, half),
            f32(far, 2, 128),
            f32(far, 2, 128),
            dma((copies,)),
            dma((copies,)),
            dma((local_rows // SPAN + 3,)),
        ],
        compiler_params=pltpu.CompilerParams(
            collective_id=0, has_side_effects=True, vmem_limit_bytes=VMEM_BYTES
        ),
        name="fused",
    )(
        cache_rows[0].T,
        cache_request,
        sent_rows.T,
        sent_owner.reshape(1, send),
        sent_request.reshape(1, send),
        jnp.transpose(new_rows, (1, 0, 2)),
        query_nope,
        query_rope,
        absorb_key,
        absorb_value,
    )


def solution(mesh):
    placed = (
        P("role", "seq", None),
        P("role", "seq"),
        P(("role", "seq"), None),
        P(("role", "seq"), None),
        P(("role", "seq")),
        P(None, "role", None),
        P(None, "role", "seq", None),
        P(None, "role", "seq", None),
        P("seq", None, None),
        P("seq", None, None),
    )
    return jax.shard_map(
        per_device,
        mesh=mesh,
        in_specs=placed,
        out_specs=P(None, "role", "seq", None),
        check_vma=False,
    )
```
